32 devices in a mesh: grp: 4 (over y, x), dev: 8 (over z, core).
Axes of the slice: x: 2, y: 2, z: 4, core: 2. Of those that a mesh axis runs over, the one named last changes fastest.
Arguments:
- phi: bfloat16 [256, 8192], P(('grp', 'dev')), may hold values from -6 to 6
- conf: float32 [256], P(('grp', 'dev')), may hold values from 0.5 to 8
- shift_energy: float32 [256], P(('grp', 'dev')), may hold values from 0.5 to 3
- kern: float32 [256, 80], P(('grp', 'dev')), may hold values from -2 to 2
- margins: int32 [256, 8], P(('grp', 'dev')), may hold values from 0 to 255, as said below
- offsets: int32 [256, 3], replicated, may hold values from 0 to 8
Outputs:
- gradient: float32 [256, 8192], P(('grp', 'dev'))
- updated: bfloat16 [256, 8192], P(('grp', 'dev'))
The draws below stay inside these ranges and needn't reach their ends.
Inputs may be any that keep to these rules, and one draw needn't show every extreme that they name: `margins`: the 8 entries of a row are distinct; at most two of them lie outside the row's group, and those belong to the function's device index in the group just below or just above.
All inputs are finite; a program needn't handle non-finite values.
Results may differ from the reference program's by a relative error of at most 0.0039.
Values may be sent and summed in bfloat16 or wider, within the bound.
A program may use at most 64 MiB of HBM per device.

```python
import math
import jax
import jax.numpy as jnp
from jax import lax

BX = 16
BY = 16
BZ = 32
NB = 8
FN_DEV = 8
R = 8192
GF = 64
FUNCS = 256
KW = 80


def draw_margins(key, part):
    groups = FUNCS // GF
    ident = jnp.arange(FUNCS, dtype=jnp.int32)
    group_of = ident // GF
    device_of = ident % GF // FN_DEV
    key_one, key_two, key_three = jax.random.split(key, 3)
    scores = jax.random.randint(key_one, (FUNCS, GF), 0, 1 << 20, dtype=jnp.int32) * GF + jnp.arange(GF, dtype=jnp.int32)[None, :]
    _, chosen = lax.top_k(scores, NB)
    inner = group_of[:, None] * GF + chosen.astype(jnp.int32)
    below = (group_of - 1) * GF + device_of * FN_DEV + jax.random.randint(key_two, (FUNCS,), 0, FN_DEV, dtype=jnp.int32)
    above = (group_of + 1) * GF + device_of * FN_DEV + jax.random.randint(key_three, (FUNCS,), 0, FN_DEV, dtype=jnp.int32)
    below = jnp.where(group_of > 0, below, inner[:, NB - 2])
    above = jnp.where(group_of < groups - 1, above, inner[:, NB - 1])
    return jnp.concatenate([inner[:, :NB - 2], below[:, None], above[:, None]], axis=1).astype(jnp.int32)


def touch_ends(values, key, least, largest):
    longest = values.shape.index(max(values.shape))
    spots = []
    for shift in (0, 1):
        where = [jax.random.randint(jax.random.fold_in(key, axis), (), 0, length) for axis, length in enumerate(values.shape)]
        where[longest] = (where[longest] + shift) % values.shape[longest]
        spots.append(tuple(where))
    return values.at[spots[0]].set(least).at[spots[1]].set(largest)


def block_scale(key, shape, cuts, smallest, largest):
    loudness, own = 1.0, jax.random.fold_in(key, 6)
    for axis_at, parts in cuts:
        draws = jnp.exp(jax.random.uniform(jax.random.fold_in(own, axis_at), (parts,), jnp.float32, smallest / len(cuts), largest / len(cuts)))
        loudness = loudness * jnp.repeat(draws, shape[axis_at] // parts).reshape([-1 if axis == axis_at else 1 for axis in range(len(shape))])
    return loudness


def noise(rng, shape, width, limit, cuts=(), held_as=jnp.bfloat16):
    factor_of = block_scale(rng, shape, cuts, -0.22, 0.18) if cuts else 1.0
    array = jax.random.normal(rng, shape, jnp.float32) * width * factor_of
    return jnp.minimum(jnp.maximum(array, -limit), limit).astype(held_as)


def setup_inputs(seed: int = 0) -> dict:
    key_list = jax.random.split(jax.random.key(seed), 7)
    phi = noise(key_list[0], (FUNCS, R), 1.0, 6.0, ((0, 32),))
    conf = jnp.clip(jnp.exp(math.log(8.0) - 2.7725887 * jax.random.uniform(key_list[1], (FUNCS,), jnp.float32) ** block_scale(key_list[1], (FUNCS,), ((0, 32),), -0.2, 0.2)), 0.5, 8.0)
    shift_energy = jnp.clip(0.5 + 2.5 * jax.random.uniform(key_list[2], (FUNCS,), jnp.float32) ** block_scale(key_list[2], (FUNCS,), ((0, 32),), -0.2, 0.2), 0.5, 3.0)
    kern = noise(key_list[3], (FUNCS, KW), 0.35, 2.0, ((0, 32),), jnp.float32)
    margins = draw_margins(jax.random.fold_in(key_list[6], 71), 0)
    offsets = touch_ends(jax.random.randint(key_list[5], (FUNCS, 3), 0, BX // 2 + 1), jax.random.fold_in(key_list[5], 1), 0, (BX // 2 + 1) - 1).astype(jnp.int32)
    return {"phi": phi, "conf": conf, "shift_energy": shift_energy, "kern": kern, "margins": margins, "offsets": offsets}


def apply_ham(phi, conf, shift_energy):
    count = phi.shape[0]
    field = phi.astype(jnp.float32).reshape(count, BX, BY, BZ)
    padded = jnp.pad(field, ((0, 0), (1, 1), (1, 1), (1, 1)))
    lap = padded[:, 2:, 1:-1, 1:-1] + padded[:, :-2, 1:-1, 1:-1]
    lap = lap + padded[:, 1:-1, 2:, 1:-1] + padded[:, 1:-1, :-2, 1:-1]
    lap = lap + padded[:, 1:-1, 1:-1, 2:] + padded[:, 1:-1, 1:-1, :-2] - 6.0 * field
    coord_x = (jnp.arange(BX, dtype=jnp.float32) - (BX - 1) / 2.0) / BX
    coord_y = (jnp.arange(BY, dtype=jnp.float32) - (BY - 1) / 2.0) / BY
    coord_z = (jnp.arange(BZ, dtype=jnp.float32) - (BZ - 1) / 2.0) / BZ
    radius = coord_x[:, None, None] ** 2 + coord_y[None, :, None] ** 2 + coord_z[None, None, :] ** 2
    value = -0.5 * lap + conf[:, None, None, None] * radius[None] * field - shift_energy[:, None, None, None] * field
    return value.reshape(count, BX * BY * BZ).astype(jnp.bfloat16)

def onehot_ref(size, delta):
    steps = jnp.arange(size, dtype=jnp.int32)
    return (steps[None, None, :] == steps[None, :, None] + delta[:, None, None]).astype(jnp.float32)

def reference(phi, conf, shift_energy, kern, margins, offsets):
    blocks = FUNCS // GF
    u_all = lax.map(lambda item: apply_ham(item[0], item[1], item[2]), (phi.reshape(blocks, GF, -1), conf.reshape(blocks, GF), shift_energy.reshape(blocks, GF)))
    u_all = u_all.reshape(FUNCS, -1)

    def one(index):
        others = margins[index]
        pieces = u_all[others].astype(jnp.float32).reshape(NB, BX, BY, BZ)
        delta = offsets[index][None, :] - offsets[others]
        group_a = index // GF
        group_b = others // GF
        col = jnp.where(group_a == group_b, others - group_b * GF, jnp.where(group_b == group_a - 1, GF + others % FN_DEV, GF + FN_DEV + others % FN_DEV))
        weight = kern[index][col.astype(jnp.int32)]
        moved = jnp.einsum('pxX,pXyz->pxyz', onehot_ref(BX, delta[:, 0]), pieces)
        moved = jnp.einsum('pyY,pxYz->pxyz', onehot_ref(BY, delta[:, 1]), moved)
        moved = jnp.einsum('pzZ,pxyZ->pxyz', onehot_ref(BZ, delta[:, 2]), moved)
        return lax.optimization_barrier(jnp.sum(weight[:, None, None, None] * moved, axis=0)).reshape(-1)
    gradient = lax.map(one, jnp.arange(FUNCS, dtype=jnp.int32))
    stepped = phi.astype(jnp.float32) - 0.5 * gradient
    scale = lax.rsqrt(lax.optimization_barrier(jnp.mean(stepped * stepped, axis=1, keepdims=True)) + 1e-06)
    return (gradient, (stepped * scale).astype(jnp.bfloat16))
```

```python
import functools

import jax
import jax.numpy as jnp
from jax import lax
from jax.experimental import pallas as pl
from jax.experimental.pallas import tpu as pltpu
from jax.sharding import PartitionSpec as P

BX = 16
BY = 16
BZ = 32
LANES = 128
YL = LANES // BZ
YT = BY // YL
ROWS = BX * YT
CHUNKS = 2
MESH = pl.DeviceIdType.MESH


def column(count, scalar_of):
    sub = lax.broadcasted_iota(jnp.int32, (count, LANES), 0)
    out = jnp.full((count, LANES), scalar_of(0))
    for f in range(1, count):
        out = jnp.where(sub == f, scalar_of(f), out)
    return out


def tile_roll(get, put, off_x, off_y, off_z, back):
    shape = off_x.shape
    lane = lax.broadcasted_iota(jnp.int32, shape, 1)
    yl, zz = lane // BZ, lane % BZ
    if back:
        off_x, off_y, off_z = (BX - off_x) % BX, (BY - off_y) % BY, (BZ - off_z) % BZ
    y_lo, y_hi = off_y % YL, off_y // YL
    index = (yl + YL - y_lo) % YL * BZ + (zz + BZ - off_z) % BZ
    carried = yl < y_lo
    y_bits = [(1 << i, (y_hi >> i) % 2 == 1) for i in range(YT.bit_length() - 1)]
    x_bits = [(1 << i, (off_x >> i) % 2 == 1) for i in range(BX.bit_length() - 1)]
    planes = []
    for x in range(BX):
        rows = [jnp.take_along_axis(get(x * YT + t), index, axis=1) for t in range(YT)]
        rows = [jnp.where(carried, rows[(t - 1) % YT], rows[t]) for t in range(YT)]
        for step, on in y_bits:
            rows = [jnp.where(on, rows[(t - step) % YT], rows[t]) for t in range(YT)]
        planes.append(rows)
    for t in range(YT):
        rows = [planes[x][t] for x in range(BX)]
        for step, on in x_bits:
            rows = [jnp.where(on, rows[(x - step) % BX], rows[x]) for x in range(BX)]
        for x in range(BX):
            put(x * YT + t, rows[x])


def kernel(
    groups,
    devs,
    phi_ref,
    conf_ref,
    shift_ref,
    kern_ref,
    margins_ref,
    offsets_ref,
    grad_ref,
    upd_ref,
    gath,
    flat,
    work,
    masks,
    cols,
    send_sem,
    recv_sem,
    halo_send,
):
    fns = phi_ref.shape[0]
    near = margins_ref.shape[1]
    per_group = devs * fns
    nz = devs // 2
    part = fns // CHUNKS
    gi = lax.axis_index("grp")
    me = lax.axis_index("dev")
    core, z = me % 2, me // 2
    sib = me + 1 - 2 * core
    base = (gi * devs + me) * fns

    barrier = pltpu.get_barrier_semaphore()
    links = (
        (z >= 0, (gi, sib)),
        (z > 0, (gi, me - 2)),
        (z < nz - 1, (gi, me + 2)),
        (gi > 0, (gi - 1, me)),
        (gi < groups - 1, (gi + 1, me)),
    )
    for here, target in links:
        @pl.when(here)
        def _():
            pl.semaphore_signal(barrier, inc=1, device_id=target, device_id_type=MESH)

    off = [column(fns, lambda f, c=c: offsets_ref[c, base + f]) for c in range(3)]
    conf = column(fns, lambda f: conf_ref[f])
    shift = column(fns, lambda f: shift_ref[f])
    shape = (fns, LANES)
    lane = lax.broadcasted_iota(jnp.int32, shape, 1)
    yl, zz = lane // BZ, lane % BZ
    zf = (zz.astype(jnp.float32) - (BZ - 1) / 2.0) / BZ
    zero = jnp.zeros(shape, jnp.float32)

    def phi_row(t):
        return phi_ref[:, t * LANES : (t + 1) * LANES].astype(jnp.float32)

    for x in range(BX):
        xf = ((x - (BX - 1) / 2.0) / BX) ** 2
        rows = [phi_row(x * YT + t) for t in range(YT)]
        ups = [pltpu.roll(r, LANES - BZ, 1) for r in rows] + [zero]
        downs = [zero] + [pltpu.roll(r, BZ, 1) for r in rows]
        for t in range(YT):
            field = rows[t]
            lap = phi_row((x + 1) * YT + t) if x < BX - 1 else zero
            if x > 0:
                lap = lap + phi_row((x - 1) * YT + t)
            lap = lap + jnp.where(yl < YL - 1, ups[t], ups[t + 1])
            lap = lap + jnp.where(yl > 0, downs[t + 1], downs[t])
            lap = lap + jnp.where(zz < BZ - 1, pltpu.roll(field, LANES - 1, 1), 0.0)
            lap = lap + jnp.where(zz > 0, pltpu.roll(field, 1, 1), 0.0)
            lap = lap - 6.0 * field
            yf = ((yl + t * YL).astype(jnp.float32) - (BY - 1) / 2.0) / BY
            radius = xf + yf * yf + zf * zf
            work[x * YT + t] = -0.5 * lap + conf * radius * field - shift * field

    def put_flat(t, value):
        flat[pl.ds(t, fns, stride=ROWS), :] = value

    tile_roll(lambda t: work[t], put_flat, off[0], off[1], off[2], False)
    for f in range(fns):
        gath[me * fns + f] = flat[f * ROWS : (f + 1) * ROWS, :].astype(jnp.bfloat16)

    def piece(block, c):
        return gath.at[pl.ds(block * fns + c * part, part)]

    def line(block, c, way, target):
        return pltpu.make_async_remote_copy(
            src_ref=piece(block, c),
            dst_ref=piece(block, c),
            send_sem=send_sem.at[way, block, c],
            recv_sem=recv_sem.at[block, c],
            device_id=(gi, target),
            device_id_type=MESH,
        )

    def halo(up, c):
        return pltpu.make_async_remote_copy(
            src_ref=piece(me, c),
            dst_ref=piece(devs if up else devs + 1, c),
            send_sem=halo_send.at[1 if up else 0, c],
            recv_sem=recv_sem.at[devs if up else devs + 1, c],
            device_id=(gi + 1 if up else gi - 1, me),
            device_id_type=MESH,
        )

    has_left, has_right = z > 0, z < nz - 1
    has_below, has_above = gi > 0, gi < groups - 1

    pl.semaphore_wait(barrier, 1 + sum(jnp.where(h, 1, 0) for h, _ in links[1:]))
    for c in range(CHUNKS):
        @pl.when(has_right)
        def _():
            line(me, c, 0, me + 2).start()

        @pl.when(has_left)
        def _():
            line(me, c, 1, me - 2).start()

        line(me, c, 2, sib).start()
    for c in range(CHUNKS):
        @pl.when(has_above)
        def _():
            halo(True, c).start()

        @pl.when(has_below)
        def _():
            halo(False, c).start()

    row = lax.broadcasted_iota(jnp.int32, (ROWS, LANES), 0)
    lan = lax.broadcasted_iota(jnp.int32, (ROWS, LANES), 1)
    cell = (row // YT, row % YT * YL + lan // BZ, lan % BZ)

    def make_masks(a, carry):
        for k in range(near):
            b = margins_ref[a, k]
            gb = b // per_group
            col = jnp.where(
                gb == gi,
                b - gb * per_group,
                jnp.where(gb == gi - 1, per_group, per_group + fns) + b % fns,
            )
            cols[a * near + k] = col
            keep = None
            for axis in range(3):
                oa, ob = offsets_ref[axis, base + a], offsets_ref[axis, b]
                out = (cell[axis] < jnp.minimum(oa, ob)) | (cell[axis] >= jnp.maximum(oa, ob))
                keep = out if keep is None else keep & out
            masks[a * near + k] = jnp.where(keep, kern_ref[a, col], 0.0)
        return carry

    half = fns // 2
    lax.fori_loop(0, half, make_masks, 0)

    for s in range(1, nz):
        for c in range(CHUNKS):
            @pl.when(z - s >= 0)
            def _():
                block = me - 2 * s
                line(block, c, 0, me + 2).wait_recv()

                @pl.when(has_right)
                def _():
                    line(block, c, 0, me + 2).start()

                line(block, c, 2, sib).start()

            @pl.when(z + s < nz)
            def _():
                block = me + 2 * s
                line(block, c, 1, me - 2).wait_recv()

                @pl.when(has_left)
                def _():
                    line(block, c, 1, me - 2).start()

                line(block, c, 2, sib).start()
        if s == 1:
            lax.fori_loop(half, fns, make_masks, 0)

    for block in range(nz):
        for c in range(CHUNKS):
            line(2 * block + 1 - core, c, 2, sib).wait_recv()
    for c in range(CHUNKS):
        @pl.when(has_below)
        def _():
            halo(True, c).wait_recv()

        @pl.when(has_above)
        def _():
            halo(False, c).wait_recv()

    def add_up(a, carry):
        total = None
        for k in range(near):
            term = masks[a * near + k] * gath[cols[a * near + k]].astype(jnp.float32)
            total = term if total is None else total + term
        flat[pl.ds(pl.multiple_of(a * ROWS, ROWS), ROWS), :] = total
        return carry

    lax.fori_loop(0, fns, add_up, 0)

    squares = [zero]

    def put_grad(t, value):
        grad_ref[:, t * LANES : (t + 1) * LANES] = value
        stepped = phi_row(t) - 0.5 * value
        work[t] = stepped
        squares[0] = squares[0] + stepped * stepped

    tile_roll(lambda t: flat[pl.ds(t, fns, stride=ROWS), :], put_grad, off[0], off[1], off[2], True)
    mean = jnp.sum(squares[0], axis=1, keepdims=True) / (ROWS * LANES)
    scale = lax.rsqrt(mean + 1e-06)
    for t in range(ROWS):
        upd_ref[:, t * LANES : (t + 1) * LANES] = (work[t] * scale).astype(jnp.bfloat16)

    for c in range(CHUNKS):
        for block in range(nz):
            line(2 * block + core, c, 2, sib).wait_send()

            @pl.when(has_right & (block <= z))
            def _():
                line(2 * block + core, c, 0, me + 2).wait_send()

            @pl.when(has_left & (block >= z))
            def _():
                line(2 * block + core, c, 1, me - 2).wait_send()

        @pl.when(has_above)
        def _():
            halo(True, c).wait_send()

        @pl.when(has_below)
        def _():
            halo(False, c).wait_send()


def on_device(groups, devs, phi, conf, shift_energy, kern, margins, offsets):
    fns, cells = phi.shape
    near = margins.shape[1]
    vmem = pl.BlockSpec(memory_space=pltpu.VMEM)
    smem = pl.BlockSpec(memory_space=pltpu.SMEM)
    return pl.pallas_call(
        functools.partial(kernel, groups, devs),
        out_shape=(
            jax.ShapeDtypeStruct((fns, cells), jnp.float32),
            jax.ShapeDtypeStruct((fns, cells), jnp.bfloat16),
        ),
        in_specs=[vmem, smem, smem, smem, smem, smem],
        out_specs=(vmem, vmem),
        scratch_shapes=[
            pltpu.VMEM(((devs + 2) * fns, ROWS, LANES), jnp.bfloat16),
            pltpu.VMEM((fns * ROWS, LANES), jnp.float32),
            pltpu.VMEM((ROWS, fns, LANES), jnp.float32),
            pltpu.VMEM((fns * near, ROWS, LANES), jnp.float32),
            pltpu.SMEM((fns * near,), jnp.int32),
            pltpu.SemaphoreType.DMA((3, devs, CHUNKS)),
            pltpu.SemaphoreType.DMA((devs + 2, CHUNKS)),
            pltpu.SemaphoreType.DMA((2, CHUNKS)),
        ],
        compiler_params=pltpu.CompilerParams(
            collective_id=0, has_side_effects=True, vmem_limit_bytes=32 * 1024 * 1024
        ),
    )(phi, conf, shift_energy, kern, margins, offsets.T)


def solution(mesh):
    in_specs = (
        P(("grp", "dev"), None),
        P(("grp", "dev")),
        P(("grp", "dev")),
        P(("grp", "dev"), None),
        P(("grp", "dev"), None),
        P(),
    )
    out_specs = (P(("grp", "dev"), None), P(("grp", "dev"), None))
    return jax.shard_map(
        functools.partial(on_device, mesh.shape["grp"], mesh.shape["dev"]),
        mesh=mesh,
        in_specs=in_specs,
        out_specs=out_specs,
        check_vma=False,
    )
```

```python
import functools

import jax
import jax.numpy as jnp
from jax import lax
from jax.experimental import pallas as pl
from jax.experimental.pallas import tpu as pltpu
from jax.sharding import PartitionSpec as P

BX = 16
BY = 16
BZ = 32
LANES = 128
YL = LANES // BZ
YT = BY // YL
ROWS = BX * YT
CHUNKS = 4
MESH = pl.DeviceIdType.MESH


def column(count, scalar_of):
    sub = lax.broadcasted_iota(jnp.int32, (count, LANES), 0)
    out = jnp.full((count, LANES), scalar_of(0))
    for f in range(1, count):
        out = jnp.where(sub == f, scalar_of(f), out)
    return out


def tile_roll(get, put, off_x, off_y, off_z, back):
    shape = off_x.shape
    lane = lax.broadcasted_iota(jnp.int32, shape, 1)
    yl, zz = lane // BZ, lane % BZ
    if back:
        off_x, off_y, off_z = (BX - off_x) % BX, (BY - off_y) % BY, (BZ - off_z) % BZ
    y_lo, y_hi = off_y % YL, off_y // YL
    index = (yl + YL - y_lo) % YL * BZ + (zz + BZ - off_z) % BZ
    carried = yl < y_lo
    y_bits = [(1 << i, (y_hi >> i) % 2 == 1) for i in range(YT.bit_length() - 1)]
    x_bits = [(1 << i, (off_x >> i) % 2 == 1) for i in range(BX.bit_length() - 1)]
    planes = []
    for x in range(BX):
        rows = [jnp.take_along_axis(get(x * YT + t), index, axis=1) for t in range(YT)]
        rows = [jnp.where(carried, rows[(t - 1) % YT], rows[t]) for t in range(YT)]
        for step, on in y_bits:
            rows = [jnp.where(on, rows[(t - step) % YT], rows[t]) for t in range(YT)]
        planes.append(rows)
    for t in range(YT):
        rows = [planes[x][t] for x in range(BX)]
        for step, on in x_bits:
            rows = [jnp.where(on, rows[(x - step) % BX], rows[x]) for x in range(BX)]
        for x in range(BX):
            put(x * YT + t, rows[x])


def kernel(
    groups,
    devs,
    phi_hbm,
    conf_hbm,
    shift_hbm,
    kern_hbm,
    margins_hbm,
    offsets_hbm,
    change_hbm,
    scale_hbm,
    *scratch,
):
    pieces = scratch[:CHUNKS]
    phi_ref, change, scale_ref, flat, work, masks = scratch[CHUNKS : CHUNKS + 6]
    conf_ref, shift_ref, kern_ref, margins_ref, offsets_ref, cols = scratch[CHUNKS + 6 : CHUNKS + 12]
    in_sem, out_sem, send_sem, recv_sem, halo_send = scratch[CHUNKS + 12 :]
    fns = phi_ref.shape[0]
    near = margins_ref.shape[1]
    per_group = devs * fns
    nz = devs // 2
    part = ROWS // CHUNKS
    gi = lax.axis_index("grp")
    me = lax.axis_index("dev")
    core, z = me % 2, me // 2
    sib = me + 1 - 2 * core
    base = (gi * devs + me) * fns

    copies = [
        pltpu.make_async_copy(src, dst, in_sem.at[i])
        for i, (src, dst) in enumerate(
            (
                (phi_hbm, phi_ref),
                (offsets_hbm, offsets_ref),
                (conf_hbm, conf_ref),
                (shift_hbm, shift_ref),
                (margins_hbm, margins_ref),
                (kern_hbm, kern_ref),
            )
        )
    ]
    for copy in copies:
        copy.start()

    barrier = pltpu.get_barrier_semaphore()
    links = (
        (z >= 0, (gi, sib)),
        (z > 0, (gi, me - 2)),
        (z < nz - 1, (gi, me + 2)),
        (gi > 0, (gi - 1, me)),
        (gi < groups - 1, (gi + 1, me)),
    )
    for here, target in links:
        @pl.when(here)
        def _():
            pl.semaphore_signal(barrier, inc=1, device_id=target, device_id_type=MESH)

    for copy in copies[:4]:
        copy.wait()

    off = [column(fns, lambda f, c=c: offsets_ref[c, base + f]) for c in range(3)]
    conf = column(fns, lambda f: conf_ref[f])
    shift = column(fns, lambda f: shift_ref[f])
    shape = (fns, LANES)
    lane = lax.broadcasted_iota(jnp.int32, shape, 1)
    yl, zz = lane // BZ, lane % BZ
    zf = (zz.astype(jnp.float32) - (BZ - 1) / 2.0) / BZ
    zero = jnp.zeros(shape, jnp.float32)

    def phi_row(t):
        return phi_ref[:, t * LANES : (t + 1) * LANES].astype(jnp.float32)

    for x in range(BX):
        xf = ((x - (BX - 1) / 2.0) / BX) ** 2
        rows = [phi_row(x * YT + t) for t in range(YT)]
        ups = [pltpu.roll(r, LANES - BZ, 1) for r in rows] + [zero]
        downs = [zero] + [pltpu.roll(r, BZ, 1) for r in rows]
        for t in range(YT):
            field = rows[t]
            lap = phi_row((x + 1) * YT + t) if x < BX - 1 else zero
            if x > 0:
                lap = lap + phi_row((x - 1) * YT + t)
            lap = lap + jnp.where(yl < YL - 1, ups[t], ups[t + 1])
            lap = lap + jnp.where(yl > 0, downs[t + 1], downs[t])
            lap = lap + jnp.where(zz < BZ - 1, pltpu.roll(field, LANES - 1, 1), 0.0)
            lap = lap + jnp.where(zz > 0, pltpu.roll(field, 1, 1), 0.0)
            lap = lap - 6.0 * field
            yf = ((yl + t * YL).astype(jnp.float32) - (BY - 1) / 2.0) / BY
            radius = xf + yf * yf + zf * zf
            work[x * YT + t] = -0.5 * lap + conf * radius * field - shift * field

    def put_flat(t, value):
        flat[pl.ds(t, fns, stride=ROWS), :] = value

    tile_roll(lambda t: work[t], put_flat, off[0], off[1], off[2], False)
    for c in range(CHUNKS):
        for f in range(fns):
            at = f * ROWS + c * part
            pieces[c][me * fns + f] = flat[at : at + part, :].astype(jnp.bfloat16)

    def piece(block, c):
        return pieces[c].at[pl.ds(block * fns, fns)]

    def line(block, c, way, target):
        return pltpu.make_async_remote_copy(
            src_ref=piece(block, c),
            dst_ref=piece(block, c),
            send_sem=send_sem.at[way, block, c],
            recv_sem=recv_sem.at[block, c],
            device_id=(gi, target),
            device_id_type=MESH,
        )

    def halo(up, c):
        return pltpu.make_async_remote_copy(
            src_ref=piece(me, c),
            dst_ref=piece(devs if up else devs + 1, c),
            send_sem=halo_send.at[1 if up else 0, c],
            recv_sem=recv_sem.at[devs if up else devs + 1, c],
            device_id=(gi + 1 if up else gi - 1, me),
            device_id_type=MESH,
        )

    has_left, has_right = z > 0, z < nz - 1
    has_below, has_above = gi > 0, gi < groups - 1

    pl.semaphore_wait(barrier, 1 + sum(jnp.where(h, 1, 0) for h, _ in links[1:]))
    for c in range(CHUNKS):
        @pl.when(has_right)
        def _():
            line(me, c, 0, me + 2).start()

        @pl.when(has_left)
        def _():
            line(me, c, 1, me - 2).start()

        line(me, c, 2, sib).start()
    for c in range(CHUNKS):
        @pl.when(has_above)
        def _():
            halo(True, c).start()

        @pl.when(has_below)
        def _():
            halo(False, c).start()
    for copy in copies[4:]:
        copy.wait()

    row = lax.broadcasted_iota(jnp.int32, (ROWS, LANES), 0)
    lan = lax.broadcasted_iota(jnp.int32, (ROWS, LANES), 1)
    cell = (row // YT, row % YT * YL + lan // BZ, lan % BZ)

    def make_masks(a, carry):
        for k in range(near):
            b = margins_ref[a, k]
            gb = b // per_group
            col = jnp.where(
                gb == gi,
                b - gb * per_group,
                jnp.where(gb == gi - 1, per_group, per_group + fns) + b % fns,
            )
            cols[a * near + k] = col
            keep = None
            for axis in range(3):
                oa, ob = offsets_ref[axis, base + a], offsets_ref[axis, b]
                out = (cell[axis] < jnp.minimum(oa, ob)) | (cell[axis] >= jnp.maximum(oa, ob))
                keep = out if keep is None else keep & out
            masks[a * near + k] = jnp.where(keep, kern_ref[a, col], 0.0)
        return carry

    def add_up(c):
        for block in range(nz):
            line(2 * block + 1 - core, c, 2, sib).wait_recv()

        @pl.when(has_below)
        def _():
            halo(True, c).wait_recv()

        @pl.when(has_above)
        def _():
            halo(False, c).wait_recv()

        def one(a, carry):
            total = None
            for k in range(near):
                mask = masks[a * near + k, c * part : (c + 1) * part]
                term = mask * pieces[c][cols[a * near + k]].astype(jnp.float32)
                total = term if total is None else total + term
            flat[pl.ds(pl.multiple_of(a * ROWS + c * part, part), part), :] = total
            return carry

        lax.fori_loop(0, fns, one, 0)

    half = fns // 2
    lax.fori_loop(0, half, make_masks, 0)

    for s in range(1, nz):
        for c in range(CHUNKS):
            @pl.when(z - s >= 0)
            def _():
                block = me - 2 * s
                line(block, c, 0, me + 2).wait_recv()

                @pl.when(has_right)
                def _():
                    line(block, c, 0, me + 2).start()

                line(block, c, 2, sib).start()

            @pl.when(z + s < nz)
            def _():
                block = me + 2 * s
                line(block, c, 1, me - 2).wait_recv()

                @pl.when(has_left)
                def _():
                    line(block, c, 1, me - 2).start()

                line(block, c, 2, sib).start()

            if s == 1 and c == CHUNKS - 1:
                lax.fori_loop(half, fns, make_masks, 0)
            if s == nz - 1 and c > 0:
                add_up(c - 1)
    add_up(CHUNKS - 1)

    squares = [zero]

    def put_change(t, value):
        value = -0.5 * value
        change[:, t * LANES : (t + 1) * LANES] = value
        stepped = phi_row(t) + value
        squares[0] = squares[0] + stepped * stepped

    tile_roll(lambda t: flat[pl.ds(t, fns, stride=ROWS), :], put_change, off[0], off[1], off[2], True)
    change_out = pltpu.make_async_copy(change, change_hbm, out_sem.at[0])
    change_out.start()
    mean = jnp.sum(squares[0], axis=1, keepdims=True) / (ROWS * LANES)
    scale = jnp.where(lane == lax.broadcasted_iota(jnp.int32, shape, 0), lax.rsqrt(mean + 1e-06), 0.0)
    scale_ref[...] = jnp.sum(scale, axis=0)[:fns]
    scale_out = pltpu.make_async_copy(scale_ref, scale_hbm, out_sem.at[1])
    scale_out.start()

    for c in range(CHUNKS):
        for block in range(nz):
            line(2 * block + core, c, 2, sib).wait_send()

            @pl.when(has_right & (block <= z))
            def _():
                line(2 * block + core, c, 0, me + 2).wait_send()

            @pl.when(has_left & (block >= z))
            def _():
                line(2 * block + core, c, 1, me - 2).wait_send()

        @pl.when(has_above)
        def _():
            halo(True, c).wait_send()

        @pl.when(has_below)
        def _():
            halo(False, c).wait_send()
    change_out.wait()
    scale_out.wait()


def on_device(groups, devs, phi, conf, shift_energy, kern, margins, offsets):
    fns, cells = phi.shape
    near = margins.shape[1]
    hbm = pl.BlockSpec(memory_space=pltpu.HBM)
    change, scale = pl.pallas_call(
        functools.partial(kernel, groups, devs),
        out_shape=(
            jax.ShapeDtypeStruct((fns, cells), jnp.float32),
            jax.ShapeDtypeStruct((fns,), jnp.float32),
        ),
        in_specs=[hbm] * 6,
        out_specs=(hbm, hbm),
        scratch_shapes=[pltpu.VMEM(((devs + 2) * fns, ROWS // CHUNKS, LANES), jnp.bfloat16)] * CHUNKS
        + [
            pltpu.VMEM((fns, cells), jnp.bfloat16),
            pltpu.VMEM((fns, cells), jnp.float32),
            pltpu.VMEM((fns,), jnp.float32),
            pltpu.VMEM((fns * ROWS, LANES), jnp.float32),
            pltpu.VMEM((ROWS, fns, LANES), jnp.float32),
            pltpu.VMEM((fns * near, ROWS, LANES), jnp.float32),
            pltpu.SMEM(conf.shape, jnp.float32),
            pltpu.SMEM(shift_energy.shape, jnp.float32),
            pltpu.SMEM(kern.shape, jnp.float32),
            pltpu.SMEM(margins.shape, jnp.int32),
            pltpu.SMEM(offsets.shape[::-1], jnp.int32),
            pltpu.SMEM((fns * near,), jnp.int32),
            pltpu.SemaphoreType.DMA((6,)),
            pltpu.SemaphoreType.DMA((2,)),
            pltpu.SemaphoreType.DMA((3, devs, CHUNKS)),
            pltpu.SemaphoreType.DMA((devs + 2, CHUNKS)),
            pltpu.SemaphoreType.DMA((2, CHUNKS)),
        ],
        compiler_params=pltpu.CompilerParams(
            collective_id=0, has_side_effects=True, vmem_limit_bytes=60 * 1024 * 1024
        ),
    )(phi, conf, shift_energy, kern, margins, offsets.T)
    gradient = -2.0 * change
    stepped = phi.astype(jnp.float32) + change
    return (gradient, (stepped * scale[:, None]).astype(jnp.bfloat16))


def solution(mesh):
    in_specs = (
        P(("grp", "dev"), None),
        P(("grp", "dev")),
        P(("grp", "dev")),
        P(("grp", "dev"), None),
        P(("grp", "dev"), None),
        P(),
    )
    out_specs = (P(("grp", "dev"), None), P(("grp", "dev"), None))
    return jax.shard_map(
        functools.partial(on_device, mesh.shape["grp"], mesh.shape["dev"]),
        mesh=mesh,
        in_specs=in_specs,
        out_specs=out_specs,
        check_vma=False,
    )
```

```python
import functools

import jax
import jax.numpy as jnp
from jax import lax
from jax.experimental import pallas as pl
from jax.experimental.pallas import tpu as pltpu
from jax.sharding import PartitionSpec as P

BX = 16
BY = 16
BZ = 32
LANES = 128
YL = LANES // BZ
YT = BY // YL
ROWS = BX * YT
CHUNKS = 4
MESH = pl.DeviceIdType.MESH


def column(count, scalar_of):
    sub = lax.broadcasted_iota(jnp.int32, (count, LANES), 0)
    out = jnp.full((count, LANES), scalar_of(0))
    for f in range(1, count):
        out = jnp.where(sub == f, scalar_of(f), out)
    return out


def tile_roll(get, put, off_x, off_y, off_z, back):
    shape = off_x.shape
    lane = lax.broadcasted_iota(jnp.int32, shape, 1)
    yl, zz = lane // BZ, lane % BZ
    if back:
        off_x, off_y, off_z = (BX - off_x) % BX, (BY - off_y) % BY, (BZ - off_z) % BZ
    y_lo, y_hi = off_y % YL, off_y // YL
    index = (yl + YL - y_lo) % YL * BZ + (zz + BZ - off_z) % BZ
    carried = yl < y_lo
    y_bits = [(1 << i, (y_hi >> i) % 2 == 1) for i in range(YT.bit_length() - 1)]
    x_bits = [(1 << i, (off_x >> i) % 2 == 1) for i in range(BX.bit_length() - 1)]
    planes = []
    for x in range(BX):
        rows = [jnp.take_along_axis(get(x * YT + t), index, axis=1) for t in range(YT)]
        rows = [jnp.where(carried, rows[(t - 1) % YT], rows[t]) for t in range(YT)]
        for step, on in y_bits:
            rows = [jnp.where(on, rows[(t - step) % YT], rows[t]) for t in range(YT)]
        planes.append(rows)
    for t in range(YT):
        rows = [planes[x][t] for x in range(BX)]
        for step, on in x_bits:
            rows = [jnp.where(on, rows[(x - step) % BX], rows[x]) for x in range(BX)]
        for x in range(BX):
            put(x * YT + t, rows[x])


def gather_kernel(groups, devs, phi_hbm, conf_hbm, shift_hbm, kern_hbm, margins_hbm, offsets_hbm, sums_ref, off_ref, phi_ref, *scratch):
    pieces = scratch[:CHUNKS]
    flat, work, masks, conf_ref, shift_ref, kern_ref, margins_ref, offsets_ref, cols = scratch[CHUNKS : CHUNKS + 9]
    in_sem, send_sem, recv_sem, halo_send = scratch[CHUNKS + 9 :]
    fns = phi_ref.shape[0]
    near = margins_ref.shape[1]
    per_group = devs * fns
    nz = devs // 2
    part = ROWS // CHUNKS
    gi = lax.axis_index("grp")
    me = lax.axis_index("dev")
    core, z = me % 2, me // 2
    sib = me + 1 - 2 * core
    base = (gi * devs + me) * fns

    copies = [
        pltpu.make_async_copy(src, dst, in_sem.at[i])
        for i, (src, dst) in enumerate(
            (
                (phi_hbm, phi_ref),
                (offsets_hbm, offsets_ref),
                (conf_hbm, conf_ref),
                (shift_hbm, shift_ref),
                (margins_hbm, margins_ref),
                (kern_hbm, kern_ref),
            )
        )
    ]
    for copy in copies:
        copy.start()

    barrier = pltpu.get_barrier_semaphore()
    links = (
        (z >= 0, (gi, sib)),
        (z > 0, (gi, me - 2)),
        (z < nz - 1, (gi, me + 2)),
        (gi > 0, (gi - 1, me)),
        (gi < groups - 1, (gi + 1, me)),
    )
    for here, target in links:
        @pl.when(here)
        def _():
            pl.semaphore_signal(barrier, inc=1, device_id=target, device_id_type=MESH)

    for copy in copies[:4]:
        copy.wait()

    off = [column(fns, lambda f, c=c: offsets_ref[c, base + f]) for c in range(3)]
    for c in range(3):
        off_ref[c] = off[c]
    conf = column(fns, lambda f: conf_ref[f])
    shift = column(fns, lambda f: shift_ref[f])
    shape = (fns, LANES)
    lane = lax.broadcasted_iota(jnp.int32, shape, 1)
    yl, zz = lane // BZ, lane % BZ
    zf = (zz.astype(jnp.float32) - (BZ - 1) / 2.0) / BZ
    zero = jnp.zeros(shape, jnp.float32)

    def phi_row(t):
        return phi_ref[:, t * LANES : (t + 1) * LANES].astype(jnp.float32)

    for x in range(BX):
        xf = ((x - (BX - 1) / 2.0) / BX) ** 2
        rows = [phi_row(x * YT + t) for t in range(YT)]
        ups = [pltpu.roll(r, LANES - BZ, 1) for r in rows] + [zero]
        downs = [zero] + [pltpu.roll(r, BZ, 1) for r in rows]
        for t in range(YT):
            field = rows[t]
            lap = phi_row((x + 1) * YT + t) if x < BX - 1 else zero
            if x > 0:
                lap = lap + phi_row((x - 1) * YT + t)
            lap = lap + jnp.where(yl < YL - 1, ups[t], ups[t + 1])
            lap = lap + jnp.where(yl > 0, downs[t + 1], downs[t])
            lap = lap + jnp.where(zz < BZ - 1, pltpu.roll(field, LANES - 1, 1), 0.0)
            lap = lap + jnp.where(zz > 0, pltpu.roll(field, 1, 1), 0.0)
            lap = lap - 6.0 * field
            yf = ((yl + t * YL).astype(jnp.float32) - (BY - 1) / 2.0) / BY
            radius = xf + yf * yf + zf * zf
            work[x * YT + t] = -0.5 * lap + conf * radius * field - shift * field

    def put_flat(t, value):
        flat[pl.ds(t, fns, stride=ROWS), :] = value

    tile_roll(lambda t: work[t], put_flat, off[0], off[1], off[2], False)
    for c in range(CHUNKS):
        for f in range(fns):
            at = f * ROWS + c * part
            pieces[c][me * fns + f] = flat[at : at + part, :].astype(jnp.bfloat16)

    def piece(block, c):
        return pieces[c].at[pl.ds(block * fns, fns)]

    def line(block, c, way, target):
        return pltpu.make_async_remote_copy(
            src_ref=piece(block, c),
            dst_ref=piece(block, c),
            send_sem=send_sem.at[way, block, c],
            recv_sem=recv_sem.at[block, c],
            device_id=(gi, target),
            device_id_type=MESH,
        )

    def halo(up, c):
        return pltpu.make_async_remote_copy(
            src_ref=piece(me, c),
            dst_ref=piece(devs if up else devs + 1, c),
            send_sem=halo_send.at[1 if up else 0, c],
            recv_sem=recv_sem.at[devs if up else devs + 1, c],
            device_id=(gi + 1 if up else gi - 1, me),
            device_id_type=MESH,
        )

    has_left, has_right = z > 0, z < nz - 1
    has_below, has_above = gi > 0, gi < groups - 1

    pl.semaphore_wait(barrier, 1 + sum(jnp.where(h, 1, 0) for h, _ in links[1:]))
    for c in range(CHUNKS):
        @pl.when(has_right)
        def _():
            line(me, c, 0, me + 2).start()

        @pl.when(has_left)
        def _():
            line(me, c, 1, me - 2).start()

        line(me, c, 2, sib).start()
    for c in range(CHUNKS):
        @pl.when(has_above)
        def _():
            halo(True, c).start()

        @pl.when(has_below)
        def _():
            halo(False, c).start()
    for copy in copies[4:]:
        copy.wait()

    row = lax.broadcasted_iota(jnp.int32, (ROWS, LANES), 0)
    lan = lax.broadcasted_iota(jnp.int32, (ROWS, LANES), 1)
    cell = (row // YT, row % YT * YL + lan // BZ, lan % BZ)

    def make_masks(a, carry):
        for k in range(near):
            b = margins_ref[a, k]
            gb = b // per_group
            col = jnp.where(
                gb == gi,
                b - gb * per_group,
                jnp.where(gb == gi - 1, per_group, per_group + fns) + b % fns,
            )
            cols[a * near + k] = col
            keep = None
            for axis in range(3):
                oa, ob = offsets_ref[axis, base + a], offsets_ref[axis, b]
                out = (cell[axis] < jnp.minimum(oa, ob)) | (cell[axis] >= jnp.maximum(oa, ob))
                keep = out if keep is None else keep & out
            masks[a * near + k] = jnp.where(keep, kern_ref[a, col], 0.0)
        return carry

    def add_up(c):
        for block in range(nz):
            line(2 * block + 1 - core, c, 2, sib).wait_recv()

        @pl.when(has_below)
        def _():
            halo(True, c).wait_recv()

        @pl.when(has_above)
        def _():
            halo(False, c).wait_recv()

        def one(a, carry):
            total = None
            for k in range(near):
                mask = masks[a * near + k, c * part : (c + 1) * part]
                term = mask * pieces[c][cols[a * near + k]].astype(jnp.float32)
                total = term if total is None else total + term
            sums_ref[pl.ds(pl.multiple_of(a * ROWS + c * part, part), part), :] = total
            return carry

        lax.fori_loop(0, fns, one, 0)

    half = fns // 2
    lax.fori_loop(0, half, make_masks, 0)

    for s in range(1, nz):
        for c in range(CHUNKS):
            @pl.when(z - s >= 0)
            def _():
                block = me - 2 * s
                line(block, c, 0, me + 2).wait_recv()

                @pl.when(has_right)
                def _():
                    line(block, c, 0, me + 2).start()

                line(block, c, 2, sib).start()

            @pl.when(z + s < nz)
            def _():
                block = me + 2 * s
                line(block, c, 1, me - 2).wait_recv()

                @pl.when(has_left)
                def _():
                    line(block, c, 1, me - 2).start()

                line(block, c, 2, sib).start()

            if s == 1 and c == CHUNKS - 1:
                lax.fori_loop(half, fns, make_masks, 0)
            if s == nz - 1 and c > 0:
                add_up(c - 1)
    add_up(CHUNKS - 1)

    for c in range(CHUNKS):
        for block in range(nz):
            line(2 * block + core, c, 2, sib).wait_send()

            @pl.when(has_right & (block <= z))
            def _():
                line(2 * block + core, c, 0, me + 2).wait_send()

            @pl.when(has_left & (block >= z))
            def _():
                line(2 * block + core, c, 1, me - 2).wait_send()

        @pl.when(has_above)
        def _():
            halo(True, c).wait_send()

        @pl.when(has_below)
        def _():
            halo(False, c).wait_send()


def step_kernel(sums_ref, off_ref, phi_ref, grad_hbm, upd_hbm, grad, upd, work, out_sem):
    fns = phi_ref.shape[0]
    squares = [jnp.zeros((fns, LANES), jnp.float32)]

    def put_grad(t, value):
        grad[:, t * LANES : (t + 1) * LANES] = value
        stepped = phi_ref[:, t * LANES : (t + 1) * LANES].astype(jnp.float32) - 0.5 * value
        work[t] = stepped
        squares[0] = squares[0] + stepped * stepped

    tile_roll(
        lambda t: sums_ref[pl.ds(t, fns, stride=ROWS), :], put_grad, off_ref[0], off_ref[1], off_ref[2], True
    )
    grad_out = pltpu.make_async_copy(grad, grad_hbm, out_sem.at[0])
    grad_out.start()
    mean = jnp.sum(squares[0], axis=1, keepdims=True) / (ROWS * LANES)
    scale = lax.rsqrt(mean + 1e-06)
    for t in range(ROWS):
        upd[:, t * LANES : (t + 1) * LANES] = (work[t] * scale).astype(jnp.bfloat16)
    upd_out = pltpu.make_async_copy(upd, upd_hbm, out_sem.at[1])
    upd_out.start()
    grad_out.wait()
    upd_out.wait()


def on_device(groups, devs, phi, conf, shift_energy, kern, margins, offsets):
    fns, cells = phi.shape
    near = margins.shape[1]
    vmem = pl.BlockSpec(memory_space=pltpu.VMEM)
    hbm = pl.BlockSpec(memory_space=pltpu.HBM)
    sums, off, held = pl.pallas_call(
        functools.partial(gather_kernel, groups, devs),
        out_shape=(
            jax.ShapeDtypeStruct((fns * ROWS, LANES), jnp.float32),
            jax.ShapeDtypeStruct((3, fns, LANES), jnp.int32),
            jax.ShapeDtypeStruct((fns, cells), jnp.bfloat16),
        ),
        in_specs=[hbm] * 6,
        out_specs=(vmem, vmem, vmem),
        scratch_shapes=[pltpu.VMEM(((devs + 2) * fns, ROWS // CHUNKS, LANES), jnp.bfloat16)] * CHUNKS
        + [
            pltpu.VMEM((fns * ROWS, LANES), jnp.float32),
            pltpu.VMEM((ROWS, fns, LANES), jnp.float32),
            pltpu.VMEM((fns * near, ROWS, LANES), jnp.float32),
            pltpu.SMEM(conf.shape, jnp.float32),
            pltpu.SMEM(shift_energy.shape, jnp.float32),
            pltpu.SMEM(kern.shape, jnp.float32),
            pltpu.SMEM(margins.shape, jnp.int32),
            pltpu.SMEM(offsets.shape[::-1], jnp.int32),
            pltpu.SMEM((fns * near,), jnp.int32),
            pltpu.SemaphoreType.DMA((6,)),
            pltpu.SemaphoreType.DMA((3, devs, CHUNKS)),
            pltpu.SemaphoreType.DMA((devs + 2, CHUNKS)),
            pltpu.SemaphoreType.DMA((2, CHUNKS)),
        ],
        compiler_params=pltpu.CompilerParams(
            collective_id=0, has_side_effects=True, vmem_limit_bytes=32 * 1024 * 1024
        ),
    )(*(
        pltpu.with_memory_space_constraint(array, pltpu.HBM)
        for array in (phi, conf, shift_energy, kern, margins, offsets.T)
    ))
    return pl.pallas_call(
        step_kernel,
        out_shape=(
            jax.ShapeDtypeStruct((fns, cells), jnp.float32),
            jax.ShapeDtypeStruct((fns, cells), jnp.bfloat16),
        ),
        in_specs=[vmem, vmem, vmem],
        out_specs=(hbm, hbm),
        scratch_shapes=[
            pltpu.VMEM((fns, cells), jnp.float32),
            pltpu.VMEM((fns, cells), jnp.bfloat16),
            pltpu.VMEM((ROWS, fns, LANES), jnp.float32),
            pltpu.SemaphoreType.DMA((2,)),
        ],
        compiler_params=pltpu.CompilerParams(vmem_limit_bytes=16 * 1024 * 1024),
    )(sums, off, held)


def solution(mesh):
    in_specs = (
        P(("grp", "dev"), None),
        P(("grp", "dev")),
        P(("grp", "dev")),
        P(("grp", "dev"), None),
        P(("grp", "dev"), None),
        P(),
    )
    out_specs = (P(("grp", "dev"), None), P(("grp", "dev"), None))
    return jax.shard_map(
        functools.partial(on_device, mesh.shape["grp"], mesh.shape["dev"]),
        mesh=mesh,
        in_specs=in_specs,
        out_specs=out_specs,
        check_vma=False,
    )
```

```python
import functools

import jax
import jax.numpy as jnp
from jax import lax
from jax.experimental import pallas as pl
from jax.experimental.pallas import tpu as pltpu
from jax.sharding import PartitionSpec as P

BX = 16
BY = 16
BZ = 32
LANES = 128
YL = LANES // BZ
YT = BY // YL
ROWS = BX * YT
CHUNKS = 4
MESH = pl.DeviceIdType.MESH


def column(count, scalar_of):
    sub = lax.broadcasted_iota(jnp.int32, (count, LANES), 0)
    out = jnp.full((count, LANES), scalar_of(0))
    for f in range(1, count):
        out = jnp.where(sub == f, scalar_of(f), out)
    return out


def tile_roll(get, put, off_x, off_y, off_z, back):
    shape = off_x.shape
    lane = lax.broadcasted_iota(jnp.int32, shape, 1)
    yl, zz = lane // BZ, lane % BZ
    if back:
        off_x, off_y, off_z = (BX - off_x) % BX, (BY - off_y) % BY, (BZ - off_z) % BZ
    y_lo, y_hi = off_y % YL, off_y // YL
    index = (yl + YL - y_lo) % YL * BZ + (zz + BZ - off_z) % BZ
    carried = yl < y_lo
    y_bits = [(1 << i, (y_hi >> i) % 2 == 1) for i in range(YT.bit_length() - 1)]
    x_bits = [(1 << i, (off_x >> i) % 2 == 1) for i in range(BX.bit_length() - 1)]
    planes = []
    for x in range(BX):
        rows = [jnp.take_along_axis(get(x * YT + t), index, axis=1) for t in range(YT)]
        rows = [jnp.where(carried, rows[(t - 1) % YT], rows[t]) for t in range(YT)]
        for step, on in y_bits:
            rows = [jnp.where(on, rows[(t - step) % YT], rows[t]) for t in range(YT)]
        planes.append(rows)
    for t in range(YT):
        rows = [planes[x][t] for x in range(BX)]
        for step, on in x_bits:
            rows = [jnp.where(on, rows[(x - step) % BX], rows[x]) for x in range(BX)]
        for x in range(BX):
            put(x * YT + t, rows[x])


def gather_kernel(groups, devs, phi_hbm, conf_hbm, shift_hbm, kern_hbm, margins_hbm, offsets_hbm, sums_ref, off_ref, phi_ref, *scratch):
    pieces = scratch[:CHUNKS]
    flat, work, masks, conf_ref, shift_ref, kern_ref, margins_ref, offsets_ref, cols = scratch[CHUNKS : CHUNKS + 9]
    far_margins_in, far_kern_in, far_margins, far_kern, far_masks, far_cols, share_out, share_in = scratch[CHUNKS + 9 : CHUNKS + 17]
    in_sem, send_sem, recv_sem, halo_send, far_send, far_recv, far_copy, share_send, share_recv = scratch[CHUNKS + 17 :]
    fns = phi_ref.shape[0]
    near = margins_ref.shape[1]
    per_group = devs * fns
    nz = devs // 2
    part = ROWS // CHUNKS
    gi = lax.axis_index("grp")
    me = lax.axis_index("dev")
    core, z = me % 2, me // 2
    sib = me + 1 - 2 * core
    base = (gi * devs + me) * fns
    at_end = (z == 0) | (z == nz - 1)
    helps = (z == 1) | (z == nz - 2)
    helped = jnp.where(z == 1, me - 2, me + 2)
    helper = jnp.where(z == 0, me + 2, me - 2)
    helped_base = (gi * devs + helped) * fns

    copies = [
        pltpu.make_async_copy(src, dst, in_sem.at[i])
        for i, (src, dst) in enumerate(
            (
                (phi_hbm, phi_ref),
                (offsets_hbm, offsets_ref),
                (conf_hbm, conf_ref),
                (shift_hbm, shift_ref),
                (margins_hbm, margins_ref),
                (kern_hbm, kern_ref),
            )
        )
    ]
    for copy in copies:
        copy.start()

    barrier = pltpu.get_barrier_semaphore()
    links = (
        (z >= 0, (gi, sib)),
        (z > 0, (gi, me - 2)),
        (z < nz - 1, (gi, me + 2)),
        (gi > 0, (gi - 1, me)),
        (gi < groups - 1, (gi + 1, me)),
    )
    for here, target in links:
        @pl.when(here)
        def _():
            pl.semaphore_signal(barrier, inc=1, device_id=target, device_id_type=MESH)

    for copy in copies[:4]:
        copy.wait()

    off = [column(fns, lambda f, c=c: offsets_ref[c, base + f]) for c in range(3)]
    for c in range(3):
        off_ref[c] = off[c]
    conf = column(fns, lambda f: conf_ref[f])
    shift = column(fns, lambda f: shift_ref[f])
    shape = (fns, LANES)
    lane = lax.broadcasted_iota(jnp.int32, shape, 1)
    yl, zz = lane // BZ, lane % BZ
    zf = (zz.astype(jnp.float32) - (BZ - 1) / 2.0) / BZ
    zero = jnp.zeros(shape, jnp.float32)

    def phi_row(t):
        return phi_ref[:, t * LANES : (t + 1) * LANES].astype(jnp.float32)

    for x in range(BX):
        xf = ((x - (BX - 1) / 2.0) / BX) ** 2
        rows = [phi_row(x * YT + t) for t in range(YT)]
        ups = [pltpu.roll(r, LANES - BZ, 1) for r in rows] + [zero]
        downs = [zero] + [pltpu.roll(r, BZ, 1) for r in rows]
        for t in range(YT):
            field = rows[t]
            lap = phi_row((x + 1) * YT + t) if x < BX - 1 else zero
            if x > 0:
                lap = lap + phi_row((x - 1) * YT + t)
            lap = lap + jnp.where(yl < YL - 1, ups[t], ups[t + 1])
            lap = lap + jnp.where(yl > 0, downs[t + 1], downs[t])
            lap = lap + jnp.where(zz < BZ - 1, pltpu.roll(field, LANES - 1, 1), 0.0)
            lap = lap + jnp.where(zz > 0, pltpu.roll(field, 1, 1), 0.0)
            lap = lap - 6.0 * field
            yf = ((yl + t * YL).astype(jnp.float32) - (BY - 1) / 2.0) / BY
            radius = xf + yf * yf + zf * zf
            work[x * YT + t] = -0.5 * lap + conf * radius * field - shift * field

    def put_flat(t, value):
        flat[pl.ds(t, fns, stride=ROWS), :] = value

    tile_roll(lambda t: work[t], put_flat, off[0], off[1], off[2], False)
    for c in range(CHUNKS):
        for f in range(fns):
            at = f * ROWS + c * part
            pieces[c][me * fns + f] = flat[at : at + part, :].astype(jnp.bfloat16)

    def piece(block, c):
        return pieces[c].at[pl.ds(block * fns, fns)]

    def line(block, c, way, target):
        return pltpu.make_async_remote_copy(
            src_ref=piece(block, c),
            dst_ref=piece(block, c),
            send_sem=send_sem.at[way, block, c],
            recv_sem=recv_sem.at[block, c],
            device_id=(gi, target),
            device_id_type=MESH,
        )

    def halo(up, c):
        return pltpu.make_async_remote_copy(
            src_ref=piece(me, c),
            dst_ref=piece(devs if up else devs + 1, c),
            send_sem=halo_send.at[1 if up else 0, c],
            recv_sem=recv_sem.at[devs if up else devs + 1, c],
            device_id=(gi + 1 if up else gi - 1, me),
            device_id_type=MESH,
        )

    has_left, has_right = z > 0, z < nz - 1
    has_below, has_above = gi > 0, gi < groups - 1

    def to_helper(i):
        src, dst = ((margins_hbm, far_margins_in), (kern_hbm, far_kern_in))[i]
        return pltpu.make_async_remote_copy(
            src_ref=src,
            dst_ref=dst,
            send_sem=far_send.at[i],
            recv_sem=far_recv.at[i],
            device_id=(gi, helper),
            device_id_type=MESH,
        )

    def to_helped(c):
        return pltpu.make_async_remote_copy(
            src_ref=share_out.at[c],
            dst_ref=share_in.at[c],
            send_sem=share_send.at[c],
            recv_sem=share_recv.at[c],
            device_id=(gi, helped),
            device_id_type=MESH,
        )

    pl.semaphore_wait(barrier, 1 + sum(jnp.where(h, 1, 0) for h, _ in links[1:]))

    @pl.when(at_end)
    def _():
        for i in range(2):
            to_helper(i).start()

    for c in range(CHUNKS):
        @pl.when(has_right)
        def _():
            line(me, c, 0, me + 2).start()

        @pl.when(has_left)
        def _():
            line(me, c, 1, me - 2).start()

        line(me, c, 2, sib).start()
    for c in range(CHUNKS):
        @pl.when(has_above)
        def _():
            halo(True, c).start()

        @pl.when(has_below)
        def _():
            halo(False, c).start()
    for copy in copies[4:]:
        copy.wait()

    row = lax.broadcasted_iota(jnp.int32, (ROWS, LANES), 0)
    lan = lax.broadcasted_iota(jnp.int32, (ROWS, LANES), 1)
    cell = (row // YT, row % YT * YL + lan // BZ, lan % BZ)

    def make_masks(far):
        rows_of, kern_of, masks_of, cols_of, first = (
            (far_margins, far_kern, far_masks, far_cols, helped_base)
            if far
            else (margins_ref, kern_ref, masks, cols, base)
        )

        def one(a, carry):
            for k in range(near):
                b = rows_of[a, k]
                gb = b // per_group
                col = jnp.where(
                    gb == gi,
                    b - gb * per_group,
                    jnp.where(gb == gi - 1, per_group, per_group + fns) + b % fns,
                )
                zb = jnp.where(gb == gi, col // (2 * fns), z)
                if far:
                    use = (gb == gi) & jnp.where(z == 1, zb >= 2, zb <= nz - 3)
                else:
                    use = ((z > 0) | (zb < 2)) & ((z < nz - 1) | (zb > nz - 3))
                col = jnp.where(use, col, me * fns)
                cols_of[a * near + k] = col
                weight = jnp.where(use, kern_of[a, col], 0.0)
                keep = None
                for axis in range(3):
                    oa, ob = offsets_ref[axis, first + a], offsets_ref[axis, b]
                    out = (cell[axis] < jnp.minimum(oa, ob)) | (cell[axis] >= jnp.maximum(oa, ob))
                    keep = out if keep is None else keep & out
                masks_of[a * near + k] = jnp.where(keep, weight, 0.0)
            return carry

        return one

    def weighted(masks_of, cols_of, a, c):
        total = None
        for k in range(near):
            mask = masks_of[a * near + k, c * part : (c + 1) * part]
            term = mask * pieces[c][cols_of[a * near + k]].astype(jnp.float32)
            total = term if total is None else total + term
        return total

    def add_up(c):
        for block in range(nz):
            @pl.when(~at_end | (abs(block - z) <= 1))
            def _():
                line(2 * block + 1 - core, c, 2, sib).wait_recv()

        @pl.when(has_below)
        def _():
            halo(True, c).wait_recv()

        @pl.when(has_above)
        def _():
            halo(False, c).wait_recv()

        def one_far(a, carry):
            share_out[c, a] = weighted(far_masks, far_cols, a, c).astype(jnp.bfloat16)
            return carry

        def one(a, carry):
            sums_ref[pl.ds(pl.multiple_of(a * ROWS + c * part, part), part), :] = weighted(masks, cols, a, c)
            return carry

        @pl.when(helps)
        def _():
            lax.fori_loop(0, fns, one_far, 0)
            to_helped(c).start()

        lax.fori_loop(0, fns, one, 0)

    half = fns // 2
    lax.fori_loop(0, half, make_masks(False), 0)

    for s in range(1, nz - 1):
        for c in range(CHUNKS):
            @pl.when((z - s >= 0) & ((z < nz - 1) | (s == 1)))
            def _():
                block = me - 2 * s
                line(block, c, 0, me + 2).wait_recv()

                @pl.when(z < nz - 2)
                def _():
                    line(block, c, 0, me + 2).start()

                line(block, c, 2, sib).start()

            @pl.when((z + s < nz) & ((z > 0) | (s == 1)))
            def _():
                block = me + 2 * s
                line(block, c, 1, me - 2).wait_recv()

                @pl.when(z > 1)
                def _():
                    line(block, c, 1, me - 2).start()

                line(block, c, 2, sib).start()

            if s == 1 and c == 0:
                lax.fori_loop(half, fns, make_masks(False), 0)
            if s == 1 and c == 1:
                @pl.when(helps)
                def _():
                    into = [
                        pltpu.make_async_copy(far_margins_in, far_margins, far_copy.at[0]),
                        pltpu.make_async_copy(far_kern_in, far_kern, far_copy.at[1]),
                    ]
                    for i in range(2):
                        to_helper(i).wait_recv()
                        into[i].start()
                    for i in range(2):
                        into[i].wait()
                    lax.fori_loop(0, half, make_masks(True), 0)

            if s == 1 and c == 2:
                @pl.when(helps)
                def _():
                    lax.fori_loop(half, fns, make_masks(True), 0)

            if s == nz - 2 and c > 0:
                add_up(c - 1)
    add_up(CHUNKS - 1)

    @pl.when(at_end)
    def _():
        for c in range(CHUNKS):
            to_helped(c).wait_recv()
            for a in range(fns):
                at = a * ROWS + c * part
                sums_ref[at : at + part, :] = sums_ref[at : at + part, :] + share_in[c, a].astype(jnp.float32)

    for c in range(CHUNKS):
        for block in range(nz):
            @pl.when(~at_end | (abs(block - z) <= 1))
            def _():
                line(2 * block + core, c, 2, sib).wait_send()

            @pl.when(has_right & ((block == z) | ((block < z) & (z < nz - 2))))
            def _():
                line(2 * block + core, c, 0, me + 2).wait_send()

            @pl.when(has_left & ((block == z) | ((block > z) & (z > 1))))
            def _():
                line(2 * block + core, c, 1, me - 2).wait_send()

        @pl.when(has_above)
        def _():
            halo(True, c).wait_send()

        @pl.when(has_below)
        def _():
            halo(False, c).wait_send()

        @pl.when(helps)
        def _():
            to_helped(c).wait_send()

    @pl.when(at_end)
    def _():
        for i in range(2):
            to_helper(i).wait_send()


def step_kernel(sums_ref, off_ref, phi_ref, grad_hbm, upd_hbm, grad, upd, work, out_sem):
    fns = phi_ref.shape[0]
    squares = [jnp.zeros((fns, LANES), jnp.float32)]

    def put_grad(t, value):
        grad[:, t * LANES : (t + 1) * LANES] = value
        stepped = phi_ref[:, t * LANES : (t + 1) * LANES].astype(jnp.float32) - 0.5 * value
        work[t] = stepped
        squares[0] = squares[0] + stepped * stepped

    tile_roll(
        lambda t: sums_ref[pl.ds(t, fns, stride=ROWS), :], put_grad, off_ref[0], off_ref[1], off_ref[2], True
    )
    grad_out = pltpu.make_async_copy(grad, grad_hbm, out_sem.at[0])
    grad_out.start()
    mean = jnp.sum(squares[0], axis=1, keepdims=True) / (ROWS * LANES)
    scale = lax.rsqrt(mean + 1e-06)
    for t in range(ROWS):
        upd[:, t * LANES : (t + 1) * LANES] = (work[t] * scale).astype(jnp.bfloat16)
    upd_out = pltpu.make_async_copy(upd, upd_hbm, out_sem.at[1])
    upd_out.start()
    grad_out.wait()
    upd_out.wait()


def on_device(groups, devs, phi, conf, shift_energy, kern, margins, offsets):
    fns, cells = phi.shape
    near = margins.shape[1]
    vmem = pl.BlockSpec(memory_space=pltpu.VMEM)
    hbm = pl.BlockSpec(memory_space=pltpu.HBM)
    sums, off, held = pl.pallas_call(
        functools.partial(gather_kernel, groups, devs),
        out_shape=(
            jax.ShapeDtypeStruct((fns * ROWS, LANES), jnp.float32),
            jax.ShapeDtypeStruct((3, fns, LANES), jnp.int32),
            jax.ShapeDtypeStruct((fns, cells), jnp.bfloat16),
        ),
        in_specs=[hbm] * 6,
        out_specs=(vmem, vmem, vmem),
        scratch_shapes=[pltpu.VMEM(((devs + 2) * fns, ROWS // CHUNKS, LANES), jnp.bfloat16)] * CHUNKS
        + [
            pltpu.VMEM((fns * ROWS, LANES), jnp.float32),
            pltpu.VMEM((ROWS, fns, LANES), jnp.float32),
            pltpu.VMEM((fns * near, ROWS, LANES), jnp.float32),
            pltpu.SMEM(conf.shape, jnp.float32),
            pltpu.SMEM(shift_energy.shape, jnp.float32),
            pltpu.SMEM(kern.shape, jnp.float32),
            pltpu.SMEM(margins.shape, jnp.int32),
            pltpu.SMEM(offsets.shape[::-1], jnp.int32),
            pltpu.SMEM((fns * near,), jnp.int32),
            pltpu.VMEM(margins.shape, jnp.int32),
            pltpu.VMEM(kern.shape, jnp.float32),
            pltpu.SMEM(margins.shape, jnp.int32),
            pltpu.SMEM(kern.shape, jnp.float32),
            pltpu.VMEM((fns * near, ROWS, LANES), jnp.float32),
            pltpu.SMEM((fns * near,), jnp.int32),
            pltpu.VMEM((CHUNKS, fns, ROWS // CHUNKS, LANES), jnp.bfloat16),
            pltpu.VMEM((CHUNKS, fns, ROWS // CHUNKS, LANES), jnp.bfloat16),
            pltpu.SemaphoreType.DMA((6,)),
            pltpu.SemaphoreType.DMA((3, devs, CHUNKS)),
            pltpu.SemaphoreType.DMA((devs + 2, CHUNKS)),
            pltpu.SemaphoreType.DMA((2, CHUNKS)),
            pltpu.SemaphoreType.DMA((2,)),
            pltpu.SemaphoreType.DMA((2,)),
            pltpu.SemaphoreType.DMA((2,)),
            pltpu.SemaphoreType.DMA((CHUNKS,)),
            pltpu.SemaphoreType.DMA((CHUNKS,)),
        ],
        compiler_params=pltpu.CompilerParams(
            collective_id=0, has_side_effects=True, vmem_limit_bytes=32 * 1024 * 1024
        ),
    )(*(
        pltpu.with_memory_space_constraint(array, pltpu.HBM)
        for array in (phi, conf, shift_energy, kern, margins, offsets.T)
    ))
    return pl.pallas_call(
        step_kernel,
        out_shape=(
            jax.ShapeDtypeStruct((fns, cells), jnp.float32),
            jax.ShapeDtypeStruct((fns, cells), jnp.bfloat16),
        ),
        in_specs=[vmem, vmem, vmem],
        out_specs=(hbm, hbm),
        scratch_shapes=[
            pltpu.VMEM((fns, cells), jnp.float32),
            pltpu.VMEM((fns, cells), jnp.bfloat16),
            pltpu.VMEM((ROWS, fns, LANES), jnp.float32),
            pltpu.SemaphoreType.DMA((2,)),
        ],
        compiler_params=pltpu.CompilerParams(vmem_limit_bytes=16 * 1024 * 1024),
    )(sums, off, held)


def solution(mesh):
    in_specs = (
        P(("grp", "dev"), None),
        P(("grp", "dev")),
        P(("grp", "dev")),
        P(("grp", "dev"), None),
        P(("grp", "dev"), None),
        P(),
    )
    out_specs = (P(("grp", "dev"), None), P(("grp", "dev"), None))
    return jax.shard_map(
        functools.partial(on_device, mesh.shape["grp"], mesh.shape["dev"]),
        mesh=mesh,
        in_specs=in_specs,
        out_specs=out_specs,
        check_vma=False,
    )
```

```python
import functools

import jax
import jax.numpy as jnp
from jax import lax
from jax.experimental import pallas as pl
from jax.experimental.pallas import tpu as pltpu
from jax.sharding import PartitionSpec as P

BX = 16
BY = 16
BZ = 32
LANES = 128
YL = LANES // BZ
YT = BY // YL
ROWS = BX * YT
CHUNKS = 4
TOP = 8
MASKED = TOP * YT
MESH = pl.DeviceIdType.MESH


def column(count, scalar_of):
    sub = lax.broadcasted_iota(jnp.int32, (count, LANES), 0)
    out = jnp.full((count, LANES), scalar_of(0))
    for f in range(1, count):
        out = jnp.where(sub == f, scalar_of(f), out)
    return out


def tile_roll(get, put, off_x, off_y, off_z, back):
    shape = off_x.shape
    lane = lax.broadcasted_iota(jnp.int32, shape, 1)
    yl, zz = lane // BZ, lane % BZ
    if back:
        off_x, off_y, off_z = (BX - off_x) % BX, (BY - off_y) % BY, (BZ - off_z) % BZ
    y_lo, y_hi = off_y % YL, off_y // YL
    index = (yl + YL - y_lo) % YL * BZ + (zz + BZ - off_z) % BZ
    carried = yl < y_lo
    y_bits = [(1 << i, (y_hi >> i) % 2 == 1) for i in range(YT.bit_length() - 1)]
    x_bits = [(1 << i, (off_x >> i) % 2 == 1) for i in range(BX.bit_length() - 1)]
    planes = []
    for x in range(BX):
        rows = [jnp.take_along_axis(get(x * YT + t), index, axis=1) for t in range(YT)]
        rows = [jnp.where(carried, rows[(t - 1) % YT], rows[t]) for t in range(YT)]
        for step, on in y_bits:
            rows = [jnp.where(on, rows[(t - step) % YT], rows[t]) for t in range(YT)]
        planes.append(rows)
    for t in range(YT):
        rows = [planes[x][t] for x in range(BX)]
        for step, on in x_bits:
            rows = [jnp.where(on, rows[(x - step) % BX], rows[x]) for x in range(BX)]
        for x in range(BX):
            put(x * YT + t, rows[x])


def gather_kernel(groups, devs, phi_hbm, conf_hbm, shift_hbm, kern_hbm, margins_hbm, offsets_hbm, sums_ref, off_ref, phi_ref, *scratch):
    pieces = scratch[:CHUNKS]
    flat, work, masks, conf_ref, shift_ref, kern_ref, margins_ref, offsets_ref, cols = scratch[CHUNKS : CHUNKS + 9]
    far_margins_in, far_kern_in, far_margins, far_kern, far_masks, far_cols, share_out, share_in = scratch[CHUNKS + 9 : CHUNKS + 17]
    in_sem, send_sem, recv_sem, halo_send, far_send, far_recv, far_copy, share_send, share_recv = scratch[CHUNKS + 17 :]
    fns = phi_ref.shape[0]
    near = margins_ref.shape[1]
    per_group = devs * fns
    nz = devs // 2
    part = ROWS // CHUNKS
    gi = lax.axis_index("grp")
    me = lax.axis_index("dev")
    core, z = me % 2, me // 2
    sib = me + 1 - 2 * core
    base = (gi * devs + me) * fns
    at_end = (z == 0) | (z == nz - 1)
    helps = (z == 1) | (z == nz - 2)
    helped = jnp.where(z == 1, me - 2, me + 2)
    helper = jnp.where(z == 0, me + 2, me - 2)
    helped_base = (gi * devs + helped) * fns

    copies = [
        pltpu.make_async_copy(src, dst, in_sem.at[i])
        for i, (src, dst) in enumerate(
            (
                (phi_hbm, phi_ref),
                (offsets_hbm, offsets_ref),
                (conf_hbm, conf_ref),
                (shift_hbm, shift_ref),
                (margins_hbm, margins_ref),
                (kern_hbm, kern_ref),
            )
        )
    ]
    for copy in copies:
        copy.start()

    barrier = pltpu.get_barrier_semaphore()
    links = (
        (z >= 0, (gi, sib)),
        (z > 0, (gi, me - 2)),
        (z < nz - 1, (gi, me + 2)),
        (gi > 0, (gi - 1, me)),
        (gi < groups - 1, (gi + 1, me)),
    )
    for here, target in links:
        @pl.when(here)
        def _():
            pl.semaphore_signal(barrier, inc=1, device_id=target, device_id_type=MESH)

    for copy in copies[:4]:
        copy.wait()

    off = [column(fns, lambda f, c=c: offsets_ref[c, base + f]) for c in range(3)]
    for c in range(3):
        off_ref[c] = off[c]
    conf = column(fns, lambda f: conf_ref[f])
    shift = column(fns, lambda f: shift_ref[f])
    shape = (fns, LANES)
    lane = lax.broadcasted_iota(jnp.int32, shape, 1)
    yl, zz = lane // BZ, lane % BZ
    zero = jnp.zeros(shape, jnp.float32)

    def phi_row(t):
        return phi_ref[:, t * LANES : (t + 1) * LANES].astype(jnp.float32)

    zf = (zz.astype(jnp.float32) - (BZ - 1) / 2.0) / BZ
    yf = [((yl + t * YL).astype(jnp.float32) - (BY - 1) / 2.0) / BY for t in range(YT)]
    plane_coef = [conf * (y * y + zf * zf) - shift + 3.0 for y in yf]
    first_y, last_y, first_z, last_z = yl == 0, yl == YL - 1, zz == 0, zz == BZ - 1
    before, rows = [zero] * YT, [phi_row(t) for t in range(YT)]
    for x in range(BX):
        after = [phi_row((x + 1) * YT + t) for t in range(YT)] if x < BX - 1 else [zero] * YT
        ups = [pltpu.roll(r, LANES - BZ, 1) for r in rows] + [zero]
        downs = [zero] + [pltpu.roll(r, BZ, 1) for r in rows]
        x_coef = conf * ((x - (BX - 1) / 2.0) / BX) ** 2
        for t in range(YT):
            field = rows[t]
            near_x = before[t] + after[t]
            near_y = jnp.where(last_y, ups[t + 1], ups[t]) + jnp.where(first_y, downs[t], downs[t + 1])
            near_z = jnp.where(last_z, 0.0, pltpu.roll(field, LANES - 1, 1))
            near_z = near_z + jnp.where(first_z, 0.0, pltpu.roll(field, 1, 1))
            work[x * YT + t] = (plane_coef[t] + x_coef) * field - 0.5 * (near_x + near_y + near_z)
        before, rows = rows, after

    def put_flat(t, value):
        flat[pl.ds(t, fns, stride=ROWS), :] = value

    tile_roll(lambda t: work[t], put_flat, off[0], off[1], off[2], False)
    for c in range(CHUNKS):
        for f in range(fns):
            at = f * ROWS + c * part
            pieces[c][me * fns + f] = flat[at : at + part, :].astype(jnp.bfloat16)

    def piece(block, c):
        return pieces[c].at[pl.ds(block * fns, fns)]

    def line(block, c, way, target):
        return pltpu.make_async_remote_copy(
            src_ref=piece(block, c),
            dst_ref=piece(block, c),
            send_sem=send_sem.at[way, block, c],
            recv_sem=recv_sem.at[block, c],
            device_id=(gi, target),
            device_id_type=MESH,
        )

    def halo(up, c):
        return pltpu.make_async_remote_copy(
            src_ref=piece(me, c),
            dst_ref=piece(devs if up else devs + 1, c),
            send_sem=halo_send.at[1 if up else 0, c],
            recv_sem=recv_sem.at[devs if up else devs + 1, c],
            device_id=(gi + 1 if up else gi - 1, me),
            device_id_type=MESH,
        )

    has_left, has_right = z > 0, z < nz - 1
    has_below, has_above = gi > 0, gi < groups - 1

    def to_helper(i):
        src, dst = ((margins_hbm, far_margins_in), (kern_hbm, far_kern_in))[i]
        return pltpu.make_async_remote_copy(
            src_ref=src,
            dst_ref=dst,
            send_sem=far_send.at[i],
            recv_sem=far_recv.at[i],
            device_id=(gi, helper),
            device_id_type=MESH,
        )

    def to_helped(c):
        return pltpu.make_async_remote_copy(
            src_ref=share_out.at[c],
            dst_ref=share_in.at[c],
            send_sem=share_send.at[c],
            recv_sem=share_recv.at[c],
            device_id=(gi, helped),
            device_id_type=MESH,
        )

    pl.semaphore_wait(barrier, 1 + sum(jnp.where(h, 1, 0) for h, _ in links[1:]))

    @pl.when(at_end)
    def _():
        for i in range(2):
            to_helper(i).start()

    for c in range(CHUNKS):
        @pl.when(has_right)
        def _():
            line(me, c, 0, me + 2).start()

        @pl.when(has_left)
        def _():
            line(me, c, 1, me - 2).start()

        line(me, c, 2, sib).start()
    for c in range(CHUNKS):
        @pl.when(has_above)
        def _():
            halo(True, c).start()

        @pl.when(has_below)
        def _():
            halo(False, c).start()
    for copy in copies[4:]:
        copy.wait()

    sub = lax.broadcasted_iota(jnp.int32, (2 * YT, LANES), 0)
    lan = lax.broadcasted_iota(jnp.int32, (2 * YT, LANES), 1)
    y_cell, z_cell = sub % YT * YL + lan // BZ, lan % BZ
    x_cells = [sub // YT + 2 * i for i in range(TOP // 2)]
    group_first = gi * per_group

    def sides(at):
        ox, oy, oz = (offsets_ref[axis, at] for axis in range(3))
        return [x < ox for x in x_cells], y_cell < oy, z_cell < oz

    def make_masks(far):
        rows_of, kern_of, masks_of, cols_of, first = (
            (far_margins, far_kern, far_masks, far_cols, helped_base)
            if far
            else (margins_ref, kern_ref, masks, cols, base)
        )

        def one(a, carry):
            ax, ay, az = sides(first + a)
            for k in range(near):
                b = rows_of[a, k]
                col = b - group_first
                inside = (col >= 0) & (col < per_group)
                beyond = jnp.where(col < 0, per_group, per_group + fns) + lax.rem(b, fns)
                col = jnp.where(inside, col, beyond)
                if far:
                    use = inside & jnp.where(z == 1, col >= 4 * fns, col < 2 * (nz - 2) * fns)
                else:
                    use = ~inside | (((z > 0) | (col < 4 * fns)) & ((z < nz - 1) | (col >= 2 * (nz - 2) * fns)))
                col = jnp.where(use, col, me * fns)
                cols_of[a * near + k] = col
                weight = jnp.where(use, kern_of[a, col], 0.0)
                bx, by, bz = sides(b)
                rest = jnp.where((ay ^ by) | (az ^ bz), 0.0, weight)
                for i in range(TOP // 2):
                    masks_of[a * near + k, 2 * YT * i : 2 * YT * (i + 1)] = jnp.where(ax[i] ^ bx[i], 0.0, rest)
                masks_of[a * near + k, MASKED:] = rest
            return carry

        return one

    def pair_mask(masks_of, pair, c):
        if c * part < MASKED:
            return masks_of[pair, c * part : (c + 1) * part]
        return jnp.concatenate([masks_of[pair, MASKED:]] * (part // (2 * YT)), axis=0)

    def weighted(masks_of, cols_of, a, c):
        total = None
        for k in range(near):
            mask = pair_mask(masks_of, a * near + k, c)
            term = mask * pieces[c][cols_of[a * near + k]].astype(jnp.float32)
            total = term if total is None else total + term
        return total

    def add_up(c):
        for block in range(nz):
            @pl.when(~at_end | (abs(block - z) <= 1))
            def _():
                line(2 * block + 1 - core, c, 2, sib).wait_recv()

        @pl.when(has_below)
        def _():
            halo(True, c).wait_recv()

        @pl.when(has_above)
        def _():
            halo(False, c).wait_recv()

        def one_far(a, carry):
            share_out[c, a] = weighted(far_masks, far_cols, a, c).astype(jnp.bfloat16)
            return carry

        def one(a, carry):
            sums_ref[pl.ds(pl.multiple_of(a * ROWS + c * part, part), part), :] = weighted(masks, cols, a, c)
            return carry

        @pl.when(helps)
        def _():
            lax.fori_loop(0, fns, one_far, 0, unroll=4)
            to_helped(c).start()

        lax.fori_loop(0, fns, one, 0, unroll=4)

    half = fns // 2
    lax.fori_loop(0, half, make_masks(False), 0)

    for s in range(1, nz - 1):
        for c in range(CHUNKS):
            @pl.when((z - s >= 0) & ((z < nz - 1) | (s == 1)))
            def _():
                block = me - 2 * s
                line(block, c, 0, me + 2).wait_recv()

                @pl.when(z < nz - 2)
                def _():
                    line(block, c, 0, me + 2).start()

                line(block, c, 2, sib).start()

            @pl.when((z + s < nz) & ((z > 0) | (s == 1)))
            def _():
                block = me + 2 * s
                line(block, c, 1, me - 2).wait_recv()

                @pl.when(z > 1)
                def _():
                    line(block, c, 1, me - 2).start()

                line(block, c, 2, sib).start()

            if s == 1 and c == 0:
                lax.fori_loop(half, fns, make_masks(False), 0)
            if s == 1 and c == 1:
                @pl.when(helps)
                def _():
                    into = [
                        pltpu.make_async_copy(far_margins_in, far_margins, far_copy.at[0]),
                        pltpu.make_async_copy(far_kern_in, far_kern, far_copy.at[1]),
                    ]
                    for i in range(2):
                        to_helper(i).wait_recv()
                        into[i].start()
                    for i in range(2):
                        into[i].wait()
                    lax.fori_loop(0, half, make_masks(True), 0)

            if s == 1 and c == 2:
                @pl.when(helps)
                def _():
                    lax.fori_loop(half, fns, make_masks(True), 0)

            if s == nz - 2 and c > 0:
                add_up(c - 1)
    add_up(CHUNKS - 1)

    @pl.when(at_end)
    def _():
        for c in range(CHUNKS):
            to_helped(c).wait_recv()
            for a in range(fns):
                at = a * ROWS + c * part
                sums_ref[at : at + part, :] = sums_ref[at : at + part, :] + share_in[c, a].astype(jnp.float32)

    for c in range(CHUNKS):
        for block in range(nz):
            @pl.when(~at_end | (abs(block - z) <= 1))
            def _():
                line(2 * block + core, c, 2, sib).wait_send()

            @pl.when(has_right & ((block == z) | ((block < z) & (z < nz - 2))))
            def _():
                line(2 * block + core, c, 0, me + 2).wait_send()

            @pl.when(has_left & ((block == z) | ((block > z) & (z > 1))))
            def _():
                line(2 * block + core, c, 1, me - 2).wait_send()

        @pl.when(has_above)
        def _():
            halo(True, c).wait_send()

        @pl.when(has_below)
        def _():
            halo(False, c).wait_send()

        @pl.when(helps)
        def _():
            to_helped(c).wait_send()

    @pl.when(at_end)
    def _():
        for i in range(2):
            to_helper(i).wait_send()


def step_kernel(sums_ref, off_ref, phi_ref, grad_hbm, upd_hbm, grad, upd, work, out_sem):
    fns = phi_ref.shape[0]
    squares = [jnp.zeros((fns, LANES), jnp.float32)]

    def put_grad(t, value):
        grad[:, t * LANES : (t + 1) * LANES] = value
        stepped = phi_ref[:, t * LANES : (t + 1) * LANES].astype(jnp.float32) - 0.5 * value
        work[t] = stepped
        squares[0] = squares[0] + stepped * stepped

    tile_roll(
        lambda t: sums_ref[pl.ds(t, fns, stride=ROWS), :], put_grad, off_ref[0], off_ref[1], off_ref[2], True
    )
    grad_out = pltpu.make_async_copy(grad, grad_hbm, out_sem.at[0])
    grad_out.start()
    mean = jnp.sum(squares[0], axis=1, keepdims=True) / (ROWS * LANES)
    scale = lax.rsqrt(mean + 1e-06)
    for t in range(ROWS):
        upd[:, t * LANES : (t + 1) * LANES] = (work[t] * scale).astype(jnp.bfloat16)
    upd_out = pltpu.make_async_copy(upd, upd_hbm, out_sem.at[1])
    upd_out.start()
    grad_out.wait()
    upd_out.wait()


def on_device(groups, devs, phi, conf, shift_energy, kern, margins, offsets):
    fns, cells = phi.shape
    near = margins.shape[1]
    vmem = pl.BlockSpec(memory_space=pltpu.VMEM)
    hbm = pl.BlockSpec(memory_space=pltpu.HBM)
    sums, off, held = pl.pallas_call(
        functools.partial(gather_kernel, groups, devs),
        out_shape=(
            jax.ShapeDtypeStruct((fns * ROWS, LANES), jnp.float32),
            jax.ShapeDtypeStruct((3, fns, LANES), jnp.int32),
            jax.ShapeDtypeStruct((fns, cells), jnp.bfloat16),
        ),
        in_specs=[hbm] * 6,
        out_specs=(vmem, vmem, vmem),
        scratch_shapes=[pltpu.VMEM(((devs + 2) * fns, ROWS // CHUNKS, LANES), jnp.bfloat16)] * CHUNKS
        + [
            pltpu.VMEM((fns * ROWS, LANES), jnp.float32),
            pltpu.VMEM((ROWS, fns, LANES), jnp.float32),
            pltpu.VMEM((fns * near, MASKED + 2 * YT, LANES), jnp.float32),
            pltpu.SMEM(conf.shape, jnp.float32),
            pltpu.SMEM(shift_energy.shape, jnp.float32),
            pltpu.SMEM(kern.shape, jnp.float32),
            pltpu.SMEM(margins.shape, jnp.int32),
            pltpu.SMEM(offsets.shape[::-1], jnp.int32),
            pltpu.SMEM((fns * near,), jnp.int32),
            pltpu.VMEM(margins.shape, jnp.int32),
            pltpu.VMEM(kern.shape, jnp.float32),
            pltpu.SMEM(margins.shape, jnp.int32),
            pltpu.SMEM(kern.shape, jnp.float32),
            pltpu.VMEM((fns * near, MASKED + 2 * YT, LANES), jnp.float32),
            pltpu.SMEM((fns * near,), jnp.int32),
            pltpu.VMEM((CHUNKS, fns, ROWS // CHUNKS, LANES), jnp.bfloat16),
            pltpu.VMEM((CHUNKS, fns, ROWS // CHUNKS, LANES), jnp.bfloat16),
            pltpu.SemaphoreType.DMA((6,)),
            pltpu.SemaphoreType.DMA((3, devs, CHUNKS)),
            pltpu.SemaphoreType.DMA((devs + 2, CHUNKS)),
            pltpu.SemaphoreType.DMA((2, CHUNKS)),
            pltpu.SemaphoreType.DMA((2,)),
            pltpu.SemaphoreType.DMA((2,)),
            pltpu.SemaphoreType.DMA((2,)),
            pltpu.SemaphoreType.DMA((CHUNKS,)),
            pltpu.SemaphoreType.DMA((CHUNKS,)),
        ],
        compiler_params=pltpu.CompilerParams(
            collective_id=0, has_side_effects=True, vmem_limit_bytes=32 * 1024 * 1024
        ),
    )(*(
        pltpu.with_memory_space_constraint(array, pltpu.HBM)
        for array in (phi, conf, shift_energy, kern, margins, offsets.T)
    ))
    return pl.pallas_call(
        step_kernel,
        out_shape=(
            jax.ShapeDtypeStruct((fns, cells), jnp.float32),
            jax.ShapeDtypeStruct((fns, cells), jnp.bfloat16),
        ),
        in_specs=[vmem, vmem, vmem],
        out_specs=(hbm, hbm),
        scratch_shapes=[
            pltpu.VMEM((fns, cells), jnp.float32),
            pltpu.VMEM((fns, cells), jnp.bfloat16),
            pltpu.VMEM((ROWS, fns, LANES), jnp.float32),
            pltpu.SemaphoreType.DMA((2,)),
        ],
        compiler_params=pltpu.CompilerParams(vmem_limit_bytes=16 * 1024 * 1024),
    )(sums, off, held)


def solution(mesh):
    in_specs = (
        P(("grp", "dev"), None),
        P(("grp", "dev")),
        P(("grp", "dev")),
        P(("grp", "dev"), None),
        P(("grp", "dev"), None),
        P(),
    )
    out_specs = (P(("grp", "dev"), None), P(("grp", "dev"), None))
    return jax.shard_map(
        functools.partial(on_device, mesh.shape["grp"], mesh.shape["dev"]),
        mesh=mesh,
        in_specs=in_specs,
        out_specs=out_specs,
        check_vma=False,
    )
```

```python
import functools

import jax
import jax.numpy as jnp
from jax import lax
from jax.experimental import pallas as pl
from jax.experimental.pallas import tpu as pltpu
from jax.sharding import PartitionSpec as P

BX = 16
BY = 16
BZ = 32
LANES = 128
YL = LANES // BZ
YT = BY // YL
ROWS = BX * YT
CHUNKS = 4
TOP = 8
MASKED = TOP * YT
MESH = pl.DeviceIdType.MESH


def column(count, scalar_of):
    sub = lax.broadcasted_iota(jnp.int32, (count, LANES), 0)
    out = jnp.full((count, LANES), scalar_of(0))
    for f in range(1, count):
        out = jnp.where(sub == f, scalar_of(f), out)
    return out


def tile_roll(get, put, off_x, off_y, off_z, back):
    shape = off_x.shape
    lane = lax.broadcasted_iota(jnp.int32, shape, 1)
    yl, zz = lane // BZ, lane % BZ
    if back:
        off_x, off_y, off_z = (BX - off_x) % BX, (BY - off_y) % BY, (BZ - off_z) % BZ
    y_lo, y_hi = off_y % YL, off_y // YL
    index = (yl + YL - y_lo) % YL * BZ + (zz + BZ - off_z) % BZ
    carried = yl < y_lo
    y_bits = [(1 << i, (y_hi >> i) % 2 == 1) for i in range(YT.bit_length() - 1)]
    x_bits = [(1 << i, (off_x >> i) % 2 == 1) for i in range(BX.bit_length() - 1)]
    planes = []
    for x in range(BX):
        rows = [jnp.take_along_axis(get(x * YT + t), index, axis=1) for t in range(YT)]
        rows = [jnp.where(carried, rows[(t - 1) % YT], rows[t]) for t in range(YT)]
        for step, on in y_bits:
            rows = [jnp.where(on, rows[(t - step) % YT], rows[t]) for t in range(YT)]
        planes.append(rows)
    for t in range(YT):
        rows = [planes[x][t] for x in range(BX)]
        for step, on in x_bits:
            rows = [jnp.where(on, rows[(x - step) % BX], rows[x]) for x in range(BX)]
        for x in range(BX):
            put(x * YT + t, rows[x])


def gather_kernel(groups, devs, phi_hbm, conf_hbm, shift_hbm, kern_hbm, margins_hbm, offsets_hbm, sums_ref, off_ref, phi_ref, *scratch):
    pieces = scratch[:CHUNKS]
    flat, work, masks, conf_ref, shift_ref, kern_ref, margins_ref, offsets_ref, cols = scratch[CHUNKS : CHUNKS + 9]
    in_sem, send_sem, recv_sem, halo_send = scratch[CHUNKS + 9 :]
    fns = phi_ref.shape[0]
    near = margins_ref.shape[1]
    per_group = devs * fns
    nz = devs // 2
    part = ROWS // CHUNKS
    gi = lax.axis_index("grp")
    me = lax.axis_index("dev")
    core, z = me % 2, me // 2
    sib = me + 1 - 2 * core
    base = (gi * devs + me) * fns

    copies = [
        pltpu.make_async_copy(src, dst, in_sem.at[i])
        for i, (src, dst) in enumerate(
            (
                (phi_hbm, phi_ref),
                (offsets_hbm, offsets_ref),
                (conf_hbm, conf_ref),
                (shift_hbm, shift_ref),
                (margins_hbm, margins_ref),
                (kern_hbm, kern_ref),
            )
        )
    ]
    for copy in copies:
        copy.start()

    barrier = pltpu.get_barrier_semaphore()
    links = (
        (z >= 0, (gi, sib)),
        (z > 0, (gi, me - 2)),
        (z < nz - 1, (gi, me + 2)),
        (gi > 0, (gi - 1, me)),
        (gi < groups - 1, (gi + 1, me)),
    )
    for here, target in links:
        @pl.when(here)
        def _():
            pl.semaphore_signal(barrier, inc=1, device_id=target, device_id_type=MESH)

    for copy in copies[:4]:
        copy.wait()

    off = [column(fns, lambda f, c=c: offsets_ref[c, base + f]) for c in range(3)]
    for c in range(3):
        off_ref[c] = off[c]
    conf = column(fns, lambda f: conf_ref[f])
    shift = column(fns, lambda f: shift_ref[f])
    shape = (fns, LANES)
    lane = lax.broadcasted_iota(jnp.int32, shape, 1)
    yl, zz = lane // BZ, lane % BZ
    zero = jnp.zeros(shape, jnp.float32)

    def phi_row(t):
        return phi_ref[:, t * LANES : (t + 1) * LANES].astype(jnp.float32)

    zf = (zz.astype(jnp.float32) - (BZ - 1) / 2.0) / BZ
    yf = [((yl + t * YL).astype(jnp.float32) - (BY - 1) / 2.0) / BY for t in range(YT)]
    plane_coef = [conf * (y * y + zf * zf) - shift + 3.0 for y in yf]
    first_y, last_y, first_z, last_z = yl == 0, yl == YL - 1, zz == 0, zz == BZ - 1
    before, rows = [zero] * YT, [phi_row(t) for t in range(YT)]
    for x in range(BX):
        after = [phi_row((x + 1) * YT + t) for t in range(YT)] if x < BX - 1 else [zero] * YT
        ups = [pltpu.roll(r, LANES - BZ, 1) for r in rows] + [zero]
        downs = [zero] + [pltpu.roll(r, BZ, 1) for r in rows]
        x_coef = conf * ((x - (BX - 1) / 2.0) / BX) ** 2
        for t in range(YT):
            field = rows[t]
            near_x = before[t] + after[t]
            near_y = jnp.where(last_y, ups[t + 1], ups[t]) + jnp.where(first_y, downs[t], downs[t + 1])
            near_z = jnp.where(last_z, 0.0, pltpu.roll(field, LANES - 1, 1))
            near_z = near_z + jnp.where(first_z, 0.0, pltpu.roll(field, 1, 1))
            work[x * YT + t] = (plane_coef[t] + x_coef) * field - 0.5 * (near_x + near_y + near_z)
        before, rows = rows, after

    def put_flat(t, value):
        flat[pl.ds(t, fns, stride=ROWS), :] = value

    tile_roll(lambda t: work[t], put_flat, off[0], off[1], off[2], False)
    for c in range(CHUNKS):
        for f in range(fns):
            at = f * ROWS + c * part
            pieces[c][me * fns + f] = flat[at : at + part, :].astype(jnp.bfloat16)

    def piece(block, c):
        return pieces[c].at[pl.ds(block * fns, fns)]

    def line(block, c, way, target):
        return pltpu.make_async_remote_copy(
            src_ref=piece(block, c),
            dst_ref=piece(block, c),
            send_sem=send_sem.at[way, block, c],
            recv_sem=recv_sem.at[block, c],
            device_id=(gi, target),
            device_id_type=MESH,
        )

    def halo(up, c):
        return pltpu.make_async_remote_copy(
            src_ref=piece(me, c),
            dst_ref=piece(devs if up else devs + 1, c),
            send_sem=halo_send.at[1 if up else 0, c],
            recv_sem=recv_sem.at[devs if up else devs + 1, c],
            device_id=(gi + 1 if up else gi - 1, me),
            device_id_type=MESH,
        )

    has_left, has_right = z > 0, z < nz - 1
    has_below, has_above = gi > 0, gi < groups - 1

    pl.semaphore_wait(barrier, 1 + sum(jnp.where(h, 1, 0) for h, _ in links[1:]))
    for c in range(CHUNKS):
        @pl.when(has_right)
        def _():
            line(me, c, 0, me + 2).start()

        @pl.when(has_left)
        def _():
            line(me, c, 1, me - 2).start()

        line(me, c, 2, sib).start()
    for c in range(CHUNKS):
        @pl.when(has_above)
        def _():
            halo(True, c).start()

        @pl.when(has_below)
        def _():
            halo(False, c).start()
    for copy in copies[4:]:
        copy.wait()

    sub = lax.broadcasted_iota(jnp.int32, (2 * YT, LANES), 0)
    lan = lax.broadcasted_iota(jnp.int32, (2 * YT, LANES), 1)
    y_cell, z_cell = sub % YT * YL + lan // BZ, lan % BZ
    x_cells = [sub // YT + 2 * i for i in range(TOP // 2)]
    group_first = gi * per_group

    def sides(at):
        ox, oy, oz = (offsets_ref[axis, at] for axis in range(3))
        return [x < ox for x in x_cells], y_cell < oy, z_cell < oz

    def make_masks(a, carry):
        ax, ay, az = sides(base + a)
        for k in range(near):
            b = margins_ref[a, k]
            col = b - group_first
            inside = (col >= 0) & (col < per_group)
            beyond = jnp.where(col < 0, per_group, per_group + fns) + lax.rem(b, fns)
            col = jnp.where(inside, col, beyond)
            cols[a * near + k] = col
            weight = kern_ref[a, col]
            bx, by, bz = sides(b)
            rest = jnp.where((ay ^ by) | (az ^ bz), 0.0, weight)
            for i in range(TOP // 2):
                masks[a * near + k, 2 * YT * i : 2 * YT * (i + 1)] = jnp.where(ax[i] ^ bx[i], 0.0, rest)
            masks[a * near + k, MASKED:] = rest
        return carry

    def pair_mask(masks_of, pair, c):
        if c * part < MASKED:
            return masks_of[pair, c * part : (c + 1) * part]
        return jnp.concatenate([masks_of[pair, MASKED:]] * (part // (2 * YT)), axis=0)

    def add_up(c):
        for block in range(nz):
            line(2 * block + 1 - core, c, 2, sib).wait_recv()

        @pl.when(has_below)
        def _():
            halo(True, c).wait_recv()

        @pl.when(has_above)
        def _():
            halo(False, c).wait_recv()

        def one(a, carry):
            total = None
            for k in range(near):
                mask = pair_mask(masks, a * near + k, c)
                term = mask * pieces[c][cols[a * near + k]].astype(jnp.float32)
                total = term if total is None else total + term
            sums_ref[pl.ds(pl.multiple_of(a * ROWS + c * part, part), part), :] = total
            return carry

        lax.fori_loop(0, fns, one, 0, unroll=4)

    half = fns // 2
    lax.fori_loop(0, half, make_masks, 0)

    for s in range(1, nz):
        for c in range(CHUNKS):
            @pl.when(z - s >= 0)
            def _():
                block = me - 2 * s
                line(block, c, 0, me + 2).wait_recv()

                @pl.when(has_right)
                def _():
                    line(block, c, 0, me + 2).start()

                line(block, c, 2, sib).start()

            @pl.when(z + s < nz)
            def _():
                block = me + 2 * s
                line(block, c, 1, me - 2).wait_recv()

                @pl.when(has_left)
                def _():
                    line(block, c, 1, me - 2).start()

                line(block, c, 2, sib).start()

            if s == 1 and c == CHUNKS - 1:
                lax.fori_loop(half, fns, make_masks, 0)
            if s == nz - 1 and c > 0:
                add_up(c - 1)
    add_up(CHUNKS - 1)

    for c in range(CHUNKS):
        for block in range(nz):
            line(2 * block + core, c, 2, sib).wait_send()

            @pl.when(has_right & (block <= z))
            def _():
                line(2 * block + core, c, 0, me + 2).wait_send()

            @pl.when(has_left & (block >= z))
            def _():
                line(2 * block + core, c, 1, me - 2).wait_send()

        @pl.when(has_above)
        def _():
            halo(True, c).wait_send()

        @pl.when(has_below)
        def _():
            halo(False, c).wait_send()


def step_kernel(sums_ref, off_ref, phi_ref, grad_hbm, upd_hbm, grad, upd, work, out_sem):
    fns = phi_ref.shape[0]
    squares = [jnp.zeros((fns, LANES), jnp.float32)]

    def put_grad(t, value):
        grad[:, t * LANES : (t + 1) * LANES] = value
        stepped = phi_ref[:, t * LANES : (t + 1) * LANES].astype(jnp.float32) - 0.5 * value
        work[t] = stepped
        squares[0] = squares[0] + stepped * stepped

    tile_roll(
        lambda t: sums_ref[pl.ds(t, fns, stride=ROWS), :], put_grad, off_ref[0], off_ref[1], off_ref[2], True
    )
    grad_out = pltpu.make_async_copy(grad, grad_hbm, out_sem.at[0])
    grad_out.start()
    mean = jnp.sum(squares[0], axis=1, keepdims=True) / (ROWS * LANES)
    scale = lax.rsqrt(mean + 1e-06)
    for t in range(ROWS):
        upd[:, t * LANES : (t + 1) * LANES] = (work[t] * scale).astype(jnp.bfloat16)
    upd_out = pltpu.make_async_copy(upd, upd_hbm, out_sem.at[1])
    upd_out.start()
    grad_out.wait()
    upd_out.wait()


def on_device(groups, devs, phi, conf, shift_energy, kern, margins, offsets):
    fns, cells = phi.shape
    near = margins.shape[1]
    vmem = pl.BlockSpec(memory_space=pltpu.VMEM)
    hbm = pl.BlockSpec(memory_space=pltpu.HBM)
    sums, off, held = pl.pallas_call(
        functools.partial(gather_kernel, groups, devs),
        out_shape=(
            jax.ShapeDtypeStruct((fns * ROWS, LANES), jnp.float32),
            jax.ShapeDtypeStruct((3, fns, LANES), jnp.int32),
            jax.ShapeDtypeStruct((fns, cells), jnp.bfloat16),
        ),
        in_specs=[hbm] * 6,
        out_specs=(vmem, vmem, vmem),
        scratch_shapes=[pltpu.VMEM(((devs + 2) * fns, ROWS // CHUNKS, LANES), jnp.bfloat16)] * CHUNKS
        + [
            pltpu.VMEM((fns * ROWS, LANES), jnp.float32),
            pltpu.VMEM((ROWS, fns, LANES), jnp.float32),
            pltpu.VMEM((fns * near, MASKED + 2 * YT, LANES), jnp.float32),
            pltpu.SMEM(conf.shape, jnp.float32),
            pltpu.SMEM(shift_energy.shape, jnp.float32),
            pltpu.SMEM(kern.shape, jnp.float32),
            pltpu.SMEM(margins.shape, jnp.int32),
            pltpu.SMEM(offsets.shape[::-1], jnp.int32),
            pltpu.SMEM((fns * near,), jnp.int32),
            pltpu.SemaphoreType.DMA((6,)),
            pltpu.SemaphoreType.DMA((3, devs, CHUNKS)),
            pltpu.SemaphoreType.DMA((devs + 2, CHUNKS)),
            pltpu.SemaphoreType.DMA((2, CHUNKS)),
        ],
        compiler_params=pltpu.CompilerParams(
            collective_id=0, has_side_effects=True, vmem_limit_bytes=32 * 1024 * 1024
        ),
    )(*(
        pltpu.with_memory_space_constraint(array, pltpu.HBM)
        for array in (phi, conf, shift_energy, kern, margins, offsets.T)
    ))
    return pl.pallas_call(
        step_kernel,
        out_shape=(
            jax.ShapeDtypeStruct((fns, cells), jnp.float32),
            jax.ShapeDtypeStruct((fns, cells), jnp.bfloat16),
        ),
        in_specs=[vmem, vmem, vmem],
        out_specs=(hbm, hbm),
        scratch_shapes=[
            pltpu.VMEM((fns, cells), jnp.float32),
            pltpu.VMEM((fns, cells), jnp.bfloat16),
            pltpu.VMEM((ROWS, fns, LANES), jnp.float32),
            pltpu.SemaphoreType.DMA((2,)),
        ],
        compiler_params=pltpu.CompilerParams(vmem_limit_bytes=16 * 1024 * 1024),
    )(sums, off, held)


def solution(mesh):
    in_specs = (
        P(("grp", "dev"), None),
        P(("grp", "dev")),
        P(("grp", "dev")),
        P(("grp", "dev"), None),
        P(("grp", "dev"), None),
        P(),
    )
    out_specs = (P(("grp", "dev"), None), P(("grp", "dev"), None))
    return jax.shard_map(
        functools.partial(on_device, mesh.shape["grp"], mesh.shape["dev"]),
        mesh=mesh,
        in_specs=in_specs,
        out_specs=out_specs,
        check_vma=False,
    )
```
